128 devices in a mesh: zero: 16 (over z, x_hi, core), tp: 8 (over x_lo, y).
Axes of the slice: x: 4 (x_hi: 2, x_lo: 2; x = x_hi * 2 + x_lo), y: 4, z: 4, core: 2. Of those that a mesh axis runs over, the one named last changes fastest.
Arguments:
- hidden_in: bfloat16 [8192, 8192], P('zero', 'tp'), may hold values from -8 to 8
- assignment: int32 [8192], replicated, may hold values from 0 to 15, as said below
- attn_gain: bfloat16 [8192], replicated, may hold values from 0.099609375 to 1.8984375
- w_query: bfloat16 [8192, 4096], P('zero', 'tp'), may hold values from -1 to 1
- w_key: bfloat16 [8192, 1024], P('zero', 'tp'), may hold values from -1 to 1
- w_value_proj: bfloat16 [8192, 1024], P('zero', 'tp'), may hold values from -0.0625 to 0.0625
- w_out: bfloat16 [4096, 8192], P('tp', 'zero'), may hold values from -0.09375 to 0.09375
- value_head: bfloat16 [8192], replicated, may hold values from -0.0625 to 0.0625
Outputs:
- scored_hidden: bfloat16 [8192, 8192], P('zero', 'tp')
- values: float32 [8192], P('zero')
The draws below stay inside these ranges and needn't reach their ends.
Inputs may be any that keep to these rules, and one draw needn't show every extreme that they name: `assignment`: row r belongs to block r // 512; every scorer is assigned exactly 512 rows in all; the rows of one block assigned to one scorer lie next to each other; every block splits its rows over the scorers by the same multiset of counts, each at most 64, and 64 is reached by every block.
All inputs are finite; a program needn't handle non-finite values.
Results may differ from the reference program's by a relative error of at most 0.012.
Values may be sent and summed in bfloat16 or wider, within the bound.
A program may use at most 128 MiB of HBM per device.

```python
import jax
import jax.numpy as jnp
from jax import lax

D = 8192
KV_HEADS = 8
HD = 128
Q_HEADS = 32
TOK_DEV = 512
TOKENS = 8192
N_ZERO = 16
N_TP = 8


def draw_hidden_in(key, part):
    key = jax.random.fold_in(key, 11)
    first = jax.random.fold_in(key, 0)
    result = jnp.clip(jax.random.normal(first, (TOKENS, D), jnp.float32), -6.0, 6.0)
    return result.astype(jnp.bfloat16)


def draw_w_query(key, part):
    key = jax.random.fold_in(key, 12)
    first = jax.random.fold_in(key, 0)
    noise = jnp.clip(jax.random.normal(first, (D, Q_HEADS * HD), jnp.float32), -4.0, 4.0)
    result = noise
    return jnp.clip(result / jnp.sqrt(jnp.float32(D)), -1.0, 1.0).astype(jnp.bfloat16)


def draw_w_key(key, part):
    key = jax.random.fold_in(key, 13)
    noise = jnp.clip(jax.random.normal(key, (D, KV_HEADS * HD), jnp.float32), -4.0, 4.0)
    result = noise
    return jnp.clip(result / jnp.sqrt(jnp.float32(D)), -1.0, 1.0).astype(jnp.bfloat16)


def draw_assignment(key, part):
    key = jax.random.fold_in(key, 14)
    first, second, third, fourth = jax.random.split(key, 4)
    mean_rows = TOK_DEV // N_ZERO
    pair_count = (N_ZERO - 2) // 2
    shifts = jax.random.randint(first, (pair_count,), -mean_rows, mean_rows + 1)
    sizes = jnp.concatenate([jnp.array([2 * mean_rows, 0], jnp.int32), (mean_rows + shifts).astype(jnp.int32), (mean_rows - shifts).astype(jnp.int32)])
    sizes = sizes[jax.random.permutation(second, N_ZERO)]
    sigma = jax.random.permutation(third, N_ZERO)
    dest_of = (sigma[:, None] + jnp.arange(N_ZERO, dtype=jnp.int32)[None, :]) % N_ZERO
    orders = jax.vmap(lambda subkey: jax.random.permutation(subkey, N_ZERO))(jax.random.split(fourth, N_ZERO))
    run_sizes = sizes[orders]
    run_dest = jnp.take_along_axis(dest_of, orders, axis=1)
    run_ends = jnp.cumsum(run_sizes, axis=1)
    row_index = jnp.arange(TOK_DEV, dtype=jnp.int32)
    run_number = jnp.sum((run_ends[:, None, :] <= row_index[None, :, None]).astype(jnp.int32), axis=2)
    dest = jnp.take_along_axis(run_dest, run_number, axis=1)
    return dest.reshape(TOKENS).astype(jnp.int32)


def levels(key, dims, pieces, smallest, top_value):
    loudness = 1.0
    for position, blocks in pieces:
        heights = jax.random.uniform(jax.random.fold_in(jax.random.fold_in(key, 6), position), (blocks,), jnp.float32, smallest / len(pieces), top_value / len(pieces))
        loudness = loudness * jnp.repeat(jnp.exp(heights), dims[position] // blocks).reshape((-1,) + (1,) * (len(dims) - 1 - position))
    return loudness


def scatter_about(rng, extent, deviation, limit, cuts=(), kind=jnp.bfloat16):
    entries = jax.random.normal(rng, extent, jnp.float32) * deviation
    if len(cuts) > 0:
        entries = levels(rng, extent, cuts, -0.22, 0.18) * entries
    return jnp.clip(entries, min=-limit, max=limit).astype(kind)


def setup_inputs(seed: int = 0) -> dict:
    key_list = jax.random.split(jax.random.key(seed), 9)
    hidden_in = draw_hidden_in(jax.random.fold_in(key_list[8], 71), 0)
    assignment = draw_assignment(jax.random.fold_in(key_list[8], 71), 0)
    attn_gain = jnp.clip(1.0 + 0.18 * jax.random.normal(key_list[2], (D,), jnp.float32), 0.099609375, 1.8984375).astype(jnp.bfloat16)
    w_query = draw_w_query(jax.random.fold_in(key_list[8], 71), 0)
    w_key = draw_w_key(jax.random.fold_in(key_list[8], 71), 0)
    w_value_proj = scatter_about(key_list[5], (D, KV_HEADS * HD), D ** -0.5, 0.0625, ((0, 16), (1, 8)))
    w_out = scatter_about(key_list[6], (Q_HEADS * HD, D), (Q_HEADS * HD) ** -0.5, 0.09375, ((0, 8), (1, 16)))
    value_head = scatter_about(key_list[7], (D,), D ** -0.5, 0.0625)
    return {"hidden_in": hidden_in, "assignment": assignment, "attn_gain": attn_gain, "w_query": w_query, "w_key": w_key, "w_value_proj": w_value_proj, "w_out": w_out, "value_head": value_head}


EPSILON = 1e-05
ROPE_BASE = 500000.0

def rotary(projected_rows, offsets, head_dim):
    row_count = projected_rows.shape[0]
    head_count = projected_rows.shape[1] // head_dim
    half_dim = head_dim // 2
    frequency = ROPE_BASE ** (-2.0 * jnp.arange(half_dim, dtype=jnp.float32) / head_dim)
    angles = offsets.astype(jnp.float32)[:, None] * frequency[None, :]
    cosine = jnp.cos(angles)[:, None, :]
    sine_part = jnp.sin(angles)[:, None, :]
    shaped = projected_rows.reshape(row_count, head_count, head_dim)
    first_half = shaped[..., :half_dim]
    second_half = shaped[..., half_dim:]
    turned = jnp.concatenate([first_half * cosine - second_half * sine_part, second_half * cosine + first_half * sine_part], axis=-1)
    return turned.reshape(row_count, head_count * head_dim)

def attend(query_rot, key_rot, value_rows, source, kv_local, head_dim):
    row_count = query_rot.shape[0]
    query_four = query_rot.reshape(row_count, kv_local, -1, head_dim).astype(jnp.float32)
    key_three = key_rot.reshape(row_count, kv_local, head_dim).astype(jnp.float32)
    value_three = value_rows.reshape(row_count, kv_local, head_dim).astype(jnp.float32)
    scores = jnp.einsum('ikgd,jkd->kgij', query_four, key_three) * (1.0 / jnp.sqrt(jnp.float32(head_dim)))
    index_rows = jnp.arange(row_count, dtype=jnp.int32)
    allowed = (source[:, None] == source[None, :]) & (index_rows[None, :] <= index_rows[:, None])
    scores = jnp.where(allowed, scores, jnp.float32(-1e+30))
    highest = lax.optimization_barrier(jnp.max(scores, axis=-1, keepdims=True))
    weights = jnp.exp(scores - highest)
    probs = (weights / lax.optimization_barrier(jnp.sum(weights, axis=-1, keepdims=True))).astype(jnp.bfloat16)
    mixed = jnp.einsum('kgij,jkd->ikgd', probs.astype(jnp.float32), value_three)
    return mixed.astype(jnp.bfloat16).reshape(row_count, -1)

def reference(hidden_in, assignment, attn_gain, w_query, w_key, w_value_proj, w_out, value_head):
    total_rows = hidden_in.shape[0]
    index_all = jnp.arange(total_rows, dtype=jnp.int32)
    order = jnp.argsort(assignment * total_rows + index_all).astype(jnp.int32)
    packed = hidden_in[order]
    source = (order // TOK_DEV).astype(jnp.int32)
    fresh = jnp.concatenate([jnp.ones((1,), dtype=bool), source[1:] != source[:-1]]) | (index_all % TOK_DEV == 0)
    run_start = lax.cummax(jnp.where(fresh, index_all, 0), axis=0)
    offset = (index_all - run_start).astype(jnp.int32)
    wide = packed.astype(jnp.float32)
    inv_scale = lax.rsqrt(lax.optimization_barrier(jnp.mean(wide * wide, axis=1, keepdims=True)) + EPSILON)
    normed = (wide * inv_scale * attn_gain.astype(jnp.float32)).astype(jnp.bfloat16)
    query_all = rotary(jnp.dot(normed, w_query, preferred_element_type=jnp.float32), offset, HD).astype(jnp.bfloat16)
    key_all = rotary(jnp.dot(normed, w_key, preferred_element_type=jnp.float32), offset, HD).astype(jnp.bfloat16)
    value_all = jnp.dot(normed, w_value_proj, preferred_element_type=jnp.float32).astype(jnp.bfloat16)

    def one_block(operands):
        query_block, key_block, value_block, source_block = operands
        return attend(query_block, key_block, value_block, source_block, KV_HEADS, HD)
    attended = lax.map(one_block, (query_all.reshape(N_ZERO, TOK_DEV, -1), key_all.reshape(N_ZERO, TOK_DEV, -1), value_all.reshape(N_ZERO, TOK_DEV, -1), source.reshape(N_ZERO, TOK_DEV)))
    attended = attended.reshape(total_rows, -1)
    group_width = Q_HEADS * HD // N_TP
    projected = jnp.zeros((total_rows, D), jnp.float32)
    for group in range(N_TP):
        term = jnp.dot(attended[:, group * group_width:(group + 1) * group_width], w_out[group * group_width:(group + 1) * group_width], preferred_element_type=jnp.float32).astype(jnp.bfloat16)
        projected = projected + lax.optimization_barrier(term).astype(jnp.float32)
    residual = wide + projected
    squares = lax.optimization_barrier(jnp.sum(residual * residual, axis=1))
    along = lax.optimization_barrier(jnp.sum(residual * value_head.astype(jnp.float32)[None, :], axis=1))
    values = along * lax.rsqrt(squares / D + EPSILON)
    return (residual.astype(jnp.bfloat16), values)
```

```python
import jax
import jax.numpy as jnp
from jax import lax
from jax.experimental import pallas as pl
from jax.experimental.pallas import tpu as pltpu
from jax.sharding import PartitionSpec as P

HD = 128
EPSILON = 1e-05
ROPE_BASE = 500000.0
MESH = pl.DeviceIdType.MESH
ROWS = 512
FEATURES = 1024
QKV = 768
CAP = 64
H_PIECES = 4
W_PIECES = 4
A_PIECES = 2
BF16 = jnp.bfloat16
F32 = jnp.float32


def dot(a, b):
    return jnp.dot(a, b, preferred_element_type=F32)


def layer(
    hid, wq, wk, wv, wo, gain_col, slot_row, target_row, offset_col, cosine, sine, head_row,
    out, val_out,
    hg, wg, wog, att, outgoing, incoming, acc, qkv, res, sums, sums_lane,
    h_send, h_recv, w_send, w_recv, o_send, o_recv, r_send, r_recv, a_send, a_recv,
    x_send, x_recv, v_send, v_recv, local_sem,
):
    zero = lax.axis_index("zero")
    tp = lax.axis_index("tp")
    z = lax.div(zero, 4)
    xh = lax.rem(lax.div(zero, 2), 2)
    core = lax.rem(zero, 2)
    xl = lax.div(tp, 4)
    y = lax.rem(tp, 4)
    spot = lax.div(zero, 2)

    def tp_of(far, dy):
        other = lax.rem(xl + far, 2)
        return other * 4 + lax.rem(y + dy + 4, 4)

    def spot_of(far, dz):
        other = lax.rem(xh + far, 2)
        return lax.rem(z + dz + 4, 4) * 2 + other

    def tp_dev(far, dy):
        return (zero, tp_of(far, dy))

    def zero_dev(far, dz):
        return (spot_of(far, dz) * 2 + core, tp)

    sibling = (spot * 2 + (1 - core), tp)

    barrier = pltpu.get_barrier_semaphore()
    greeted = 0
    for k in range(1, 16):
        pl.semaphore_signal(barrier, inc=1, device_id=(lax.rem(zero + k, 16), tp), device_id_type=MESH)
        greeted += 1
    for k in range(1, 8):
        pl.semaphore_signal(barrier, inc=1, device_id=(zero, lax.rem(tp + k, 8)), device_id_type=MESH)
        greeted += 1
    for k in range(8):
        source = (tp * 2 + core, lax.rem(tp + k, 8))
        if k == 0:
            @pl.when(spot != tp)
            def _():
                pl.semaphore_signal(barrier, inc=1, device_id=source, device_id_type=MESH)
        else:
            pl.semaphore_signal(barrier, inc=1, device_id=source, device_id_type=MESH)

    wg[zero, :, 0:512] = (wq[...].astype(F32) * gain_col[...]).astype(BF16)
    wg[zero, :, 512:640] = (wk[...].astype(F32) * gain_col[...]).astype(BF16)
    wg[zero, :, 640:768] = (wv[...].astype(F32) * gain_col[...]).astype(BF16)

    @pl.when(spot != tp)
    def _():
        pl.semaphore_wait(barrier, greeted + 8)

    @pl.when(spot == tp)
    def _():
        pl.semaphore_wait(barrier, greeted + 7)

    started = []

    def send(src, dst, send_sem, recv_sem, device):
        copy = pltpu.make_async_remote_copy(
            src_ref=src, dst_ref=dst, send_sem=send_sem, recv_sem=recv_sem, device_id=device, device_id_type=MESH
        )
        copy.start()
        started.append(copy)

    def arrived(ref, sem):
        pltpu.make_async_remote_copy(
            src_ref=ref, dst_ref=ref, send_sem=sem, recv_sem=sem, device_id=sibling, device_id_type=MESH
        ).wait_recv()

    class Gather:
        def __init__(self, block, index_of, device_of, pieces, send_sems, recv_sems, across_relay, copy_on):
            self.block, self.index_of, self.device_of, self.pieces = block, index_of, device_of, pieces
            self.send_sems, self.recv_sems = send_sems, recv_sems
            self.across_relay, self.copy_on = across_relay, copy_on
            self.count = 0

        def push(self, index, p, device, src=None):
            dst = self.block(index, p)
            send(dst if src is None else src, dst, self.send_sems.at[self.count], self.recv_sems.at[index, p], device)
            self.count += 1

        def own(self, p, src=None):
            index = self.index_of(0, 0)
            self.push(index, p, self.device_of(1, 0), src)
            self.push(index, p, self.device_of(0, 1), src)
            self.push(index, p, self.device_of(0, -1), src)
            self.on(index, p, src)

        def on(self, index, p, src=None):
            if self.copy_on:
                self.push(index, p, sibling, src)

        def wait(self, index, p):
            arrived(self.block(index, p), self.recv_sems.at[index, p])

        def across(self, p):
            index = self.index_of(1, 0)
            self.wait(index, p)
            self.push(index, p, self.device_of(0, 1))
            self.push(index, p, self.device_of(0, -1))
            self.on(index, p)

        def line(self, far, p):
            below, above = self.index_of(far, -1), self.index_of(far, 1)
            relayed = far == 0 or not self.across_relay
            self.wait(below, p)
            if relayed and p < self.pieces // 2:
                self.push(below, p, self.device_of(0, 1))
            self.on(below, p)
            self.wait(above, p)
            if relayed and p >= self.pieces // 2:
                self.push(above, p, self.device_of(0, -1))
            self.on(above, p)

        def opposite(self, far, p):
            index = self.index_of(far, 2)
            self.wait(index, p)
            if far == 0 and self.across_relay:
                self.push(index, p, self.device_of(1, 0))
            self.on(index, p)

    def copied_on(gather):
        for far in range(2):
            for d in (0, 1, -1, 2):
                for p in range(gather.pieces):
                    index = spot_of(far, d) * 2 + (1 - core)
                    gather.wait(index, p)

    h_rows = ROWS // H_PIECES
    hidden = Gather(
        lambda index, p: hg.at[index, pl.ds(p * h_rows, h_rows)], tp_of, tp_dev, H_PIECES, h_send, h_recv, True, False
    )
    w_rows = ROWS // W_PIECES
    weights = Gather(
        lambda index, p: wg.at[index, pl.ds(p * w_rows, w_rows)],
        lambda far, dz: spot_of(far, dz) * 2 + core, zero_dev, W_PIECES, w_send, w_recv, False, True,
    )
    for p in range(max(H_PIECES, W_PIECES)):
        if p < H_PIECES:
            hidden.own(p, hid.at[pl.ds(p * h_rows, h_rows)])
        if p < W_PIECES:
            weights.own(p)
    hg[tp] = hid[...]

    for k in range(8):
        slot = lax.rem(spot + k, 8)
        rows = pl.ds(pl.multiple_of(slot * 64, 64), 64)
        src, dst = wo.at[rows], wog.at[core, tp, rows]
        copy = pltpu.make_async_remote_copy(
            src_ref=src, dst_ref=dst, send_sem=r_send.at[k], recv_sem=r_recv.at[lax.rem(tp - spot + 8, 8)],
            device_id=(slot * 2 + core, spot), device_id_type=MESH,
        )
        if k == 0:
            @pl.when(spot != tp)
            def _():
                copy.start()

            @pl.when(spot == tp)
            def _():
                pltpu.make_async_copy(src, dst, local_sem).start()
        else:
            copy.start()
            started.append(copy)

    for p in range(W_PIECES):
        if p < H_PIECES:
            hidden.across(p)
        weights.across(p)
        if p < H_PIECES:
            hidden.line(0, p)
        weights.line(0, p)
    for p in range(W_PIECES):
        if p < H_PIECES:
            hidden.opposite(0, p)
        weights.line(1, p)
        weights.opposite(0, p)

    my_rows = pl.ds(pl.multiple_of(spot * 64, 64), 64)
    for k in range(8):
        ref = wog.at[core, lax.rem(tp + k, 8), my_rows]
        if k == 0:
            @pl.when(spot != tp)
            def _():
                arrived(ref, r_recv.at[0])
                pltpu.make_async_remote_copy(
                    src_ref=wo.at[my_rows], dst_ref=ref, send_sem=r_send.at[0], recv_sem=r_recv.at[0],
                    device_id=sibling, device_id_type=MESH,
                ).wait_send()

            @pl.when(spot == tp)
            def _():
                pltpu.make_async_copy(wo.at[my_rows], ref, local_sem).wait()
        else:
            arrived(ref, r_recv.at[k])
    w_out = Gather(
        lambda index, p: wog.at[
            lax.rem(index, 2), pl.ds(p * 4, 4), pl.ds(pl.multiple_of(lax.div(index, 2) * 64, 64), 64)
        ],
        lambda far, dz: spot_of(far, dz) * 2 + core, zero_dev, 2, o_send, o_recv, False, True,
    )
    for p in range(W_PIECES):
        weights.opposite(1, p)
        if p < H_PIECES:
            hidden.line(1, p)
    for p in range(H_PIECES):
        hidden.opposite(1, p)
    for p in range(2):
        w_out.own(p)
    copied_on(weights)
    if STOP == 1:
        for p in range(2):
            w_out.across(p)
            w_out.line(0, p)
        for p in range(2):
            w_out.line(1, p)
            w_out.opposite(0, p)
        for p in range(2):
            w_out.opposite(1, p)
        copied_on(w_out)
        for copy in started:
            copy.wait_send()
        out[...] = hg[0]
        val_out[...] = jnp.zeros_like(val_out)
        return

    acc[...] = jnp.zeros_like(acc)
    sums_lane[...] = jnp.zeros_like(sums_lane)

    def project(k, carry):
        half = pl.ds(pl.multiple_of(lax.rem(k, 2) * 512, 512), 512)
        block = hg[lax.div(k, 2), :, half]
        acc[...] += dot(block, wg[k])
        wide = block.astype(F32)
        squares = wide * wide
        sums_lane[...] += squares[:, 0:128] + squares[:, 128:256] + squares[:, 256:384] + squares[:, 384:512]
        return carry

    lax.fori_loop(0, 16, project, 0)
    scale = lax.rsqrt(jnp.sum(sums_lane[...], axis=1, keepdims=True) * (1.0 / 8192) + EPSILON)
    cos, sin = cosine[...], sine[...]
    for h in range(5):
        part = acc[:, h * HD:(h + 1) * HD] * scale
        qkv[:, h * HD:(h + 1) * HD] = (part * cos + pltpu.roll(part, 64, 1) * sin).astype(BF16)
    qkv[:, 640:768] = (acc[:, 640:768] * scale).astype(BF16)

    for t in range(4):
        first = max(t * 128 - 128, 0)
        keys = qkv[first:first + 256, 512:640]
        vals = qkv[first:first + 256, 640:768]
        row = lax.broadcasted_iota(jnp.int32, (128, 256), 0) + t * 128
        col = lax.broadcasted_iota(jnp.int32, (128, 256), 1) + first
        allowed = (col <= row) & (col >= row - offset_col[t * 128:(t + 1) * 128, :])
        for h in range(4):
            query = qkv[t * 128:(t + 1) * 128, h * HD:(h + 1) * HD]
            scores = lax.dot_general(query, keys, (((1,), (1,)), ((), ())), preferred_element_type=F32)
            scores = jnp.where(allowed, scores * (HD ** -0.5), -1e30)
            weight = jnp.exp(scores - jnp.max(scores, axis=1, keepdims=True))
            probs = (weight / jnp.sum(weight, axis=1, keepdims=True)).astype(BF16)
            att[tp, t * 128:(t + 1) * 128, h * HD:(h + 1) * HD] = dot(probs, vals).astype(BF16)

    a_rows = ROWS // A_PIECES
    attended = Gather(
        lambda index, p: att.at[index, pl.ds(p * a_rows, a_rows)], tp_of, tp_dev, A_PIECES, a_send, a_recv, True, False
    )
    for p in range(A_PIECES):
        attended.own(p)
    for p in range(2):
        w_out.across(p)
        w_out.line(0, p)
    for p in range(A_PIECES):
        attended.across(p)
        attended.line(0, p)
    for p in range(2):
        w_out.line(1, p)
        w_out.opposite(0, p)
    for p in range(A_PIECES):
        attended.opposite(0, p)
    for p in range(2):
        w_out.opposite(1, p)
    for p in range(A_PIECES):
        attended.line(1, p)
    copied_on(w_out)
    for p in range(A_PIECES):
        attended.opposite(1, p)

    res[...] = hid[...].astype(F32)

    def output(k, carry):
        for c in range(2):
            res[:, c * 512:(c + 1) * 512] += dot(att[k], wog[c, k])
        return carry

    lax.fori_loop(0, 8, output, 0)

    def bucket(t, carry):
        slots = lax.broadcasted_iota(jnp.int32, (256, ROWS), 0) + t * 256
        chosen = jnp.where(slots == slot_row[...], 1.0, 0.0).astype(BF16)
        rows = dot(chosen, res[...].astype(BF16)).astype(BF16)
        outgoing[pl.ds(pl.multiple_of(t * 256, 256), 256)] = rows
        return carry

    lax.fori_loop(0, 4, bucket, 0)

    def place(index):
        return pl.ds(pl.multiple_of(index * CAP, CAP), CAP)

    for k in range(1, 16):
        to = lax.rem(zero + k, 16)
        send(outgoing.at[place(to)], incoming.at[place(zero)], x_send.at[k], x_recv.at[k], (to, tp))
    incoming[place(zero)] = outgoing[place(zero)]
    for k in range(1, 16):
        arrived(incoming.at[place(lax.rem(zero + 16 - k, 16))], x_recv.at[k])

    def unpack(t, carry):
        rows = lax.broadcasted_iota(jnp.int32, (256, 16 * CAP), 0) + t * 256
        chosen = jnp.where(rows == target_row[...], 1.0, 0.0).astype(BF16)
        out[pl.ds(pl.multiple_of(t * 256, 256), 256)] = dot(chosen, incoming[...]).astype(BF16)
        return carry

    lax.fori_loop(0, 2, unpack, 0)

    squares = jnp.zeros((ROWS, 128), F32)
    along = jnp.zeros((ROWS, 128), F32)
    for c in range(8):
        part = out[:, c * 128:(c + 1) * 128].astype(F32)
        squares = squares + part * part
        along = along + part * head_row[:, c * 128:(c + 1) * 128]
    sums[tp, 0:1, :] = jnp.sum(squares.T, axis=0, keepdims=True)
    sums[tp, 1:2, :] = jnp.sum(along.T, axis=0, keepdims=True)
    for k in range(1, 8):
        send(sums.at[tp], sums.at[tp], v_send.at[k], v_recv.at[k], (zero, lax.rem(tp + k, 8)))
    for k in range(1, 8):
        arrived(sums.at[lax.rem(tp + 8 - k, 8)], v_recv.at[k])
    total = sums[0]
    for k in range(1, 8):
        total = total + sums[k]
    val_out[...] = total[1:2] * lax.rsqrt(total[0:1] * (1.0 / 8192) + EPSILON)
    for copy in started:
        copy.wait_send()


STOP = 0


def shards(hidden_in, assignment, attn_gain, w_query, w_key, w_value_proj, w_out, value_head):
    zero = lax.axis_index("zero")
    tp = lax.axis_index("tp")
    scorers = jnp.arange(16, dtype=jnp.int32)
    rows = jnp.arange(ROWS, dtype=jnp.int32)
    places = jnp.arange(CAP, dtype=jnp.int32)
    blocks = assignment.reshape(16, ROWS)
    own = lax.dynamic_slice_in_dim(assignment, zero * ROWS, ROWS, 0)
    chosen = own[:, None] == scorers[None, :]
    first = jnp.min(jnp.where(chosen, rows[:, None], ROWS), axis=0)
    offset = rows - jnp.sum(jnp.where(chosen, first[None, :], 0), axis=1)
    slot_row = (own * CAP + offset)[None, :]
    counts = jnp.sum((blocks == zero).astype(jnp.int32), axis=1)
    starts = jnp.sum(jnp.where(scorers[None, :] < scorers[:, None], counts[None, :], 0), axis=1)
    target = jnp.where(places[None, :] < counts[:, None], starts[:, None] + places[None, :], -1).reshape(1, 16 * CAP)
    frequency = ROPE_BASE ** (-2.0 * jnp.arange(HD // 2, dtype=F32) / HD)
    angles = offset.astype(F32)[:, None] * frequency[None, :]
    cosine, sine = jnp.cos(angles), jnp.sin(angles)
    cosine = jnp.concatenate([cosine, cosine], axis=1)
    sine = jnp.concatenate([-sine, sine], axis=1)
    gain_col = lax.dynamic_slice_in_dim(attn_gain, zero * ROWS, ROWS, 0).astype(F32)[:, None]
    head_row = lax.dynamic_slice_in_dim(value_head, tp * FEATURES, FEATURES, 0).astype(F32)[None, :]
    vmem = pl.BlockSpec(memory_space=pltpu.VMEM)
    dma = pltpu.SemaphoreType.DMA
    scored, values = pl.pallas_call(
        layer,
        out_shape=(jax.ShapeDtypeStruct((ROWS, FEATURES), BF16), jax.ShapeDtypeStruct((1, ROWS), F32)),
        in_specs=[vmem] * 12,
        out_specs=(vmem, vmem),
        scratch_shapes=[
            pltpu.VMEM((8, ROWS, FEATURES), BF16),
            pltpu.VMEM((16, ROWS, QKV), BF16),
            pltpu.VMEM((2, 8, ROWS, 512), BF16),
            pltpu.VMEM((8, ROWS, 512), BF16),
            pltpu.VMEM((16 * CAP, FEATURES), BF16),
            pltpu.VMEM((16 * CAP, FEATURES), BF16),
            pltpu.VMEM((ROWS, QKV), F32),
            pltpu.VMEM((ROWS, QKV), BF16),
            pltpu.VMEM((ROWS, FEATURES), F32),
            pltpu.VMEM((8, 8, ROWS), F32),
            pltpu.VMEM((ROWS, 128), F32),
            dma((7 * H_PIECES,)), dma((8, H_PIECES)),
            dma((15 * W_PIECES,)), dma((16, W_PIECES)),
            dma((30,)), dma((16, 2)),
            dma((8,)), dma((8,)),
            dma((7 * A_PIECES,)), dma((8, A_PIECES)),
            dma((16,)), dma((16,)),
            dma((8,)), dma((8,)),
            dma,
        ],
        compiler_params=pltpu.CompilerParams(
            collective_id=0, has_side_effects=True, vmem_limit_bytes=58 * 2**20
        ),
        name="layer",
    )(
        hidden_in, w_query, w_key, w_value_proj, w_out, gain_col, slot_row, target, offset[:, None], cosine, sine,
        head_row,
    )
    return scored, values.reshape(ROWS)


def solution(mesh):
    in_specs = (P("zero", "tp"), P(), P(), P("zero", "tp"), P("zero", "tp"), P("zero", "tp"), P("tp", "zero"), P())
    return jax.shard_map(
        shards, mesh=mesh, in_specs=in_specs, out_specs=(P("zero", "tp"), P("zero")), check_vma=False
    )
```

```python
import jax
import jax.numpy as jnp
import numpy as np
from jax import lax
from jax.experimental import pallas as pl
from jax.experimental.pallas import tpu as pltpu
from jax.sharding import PartitionSpec as P

HD = 128
EPSILON = 1e-05
ROPE_BASE = 500000.0
MESH = pl.DeviceIdType.MESH
ROWS = 512
FEATURES = 1024
QKV = 768
CAP = 64
H_PIECES = 4
W_PIECES = 4
A_PIECES = 4
BF16 = jnp.bfloat16
F32 = jnp.float32


def dot(a, b):
    return jnp.dot(a, b, preferred_element_type=F32)


def layer(
    hid, assignment, gain, head, wq, wk, wv, wo, table,
    out, val_out,
    hg, wg, wog, att, outgoing, incoming, acc, qkv, res, sums, lanes, blocks, turns, runs, packed_values, got_values, dealt,
    h_send, h_recv, w_send, w_recv, o_send, o_recv, r_send, r_recv, a_send, a_recv,
    x_send, x_recv, v_send, v_recv, y_send, y_recv, q_send, q_recv,
):
    zero = lax.axis_index("zero")
    tp = lax.axis_index("tp")
    z = lax.div(zero, 4)
    xh = lax.rem(lax.div(zero, 2), 2)
    core = lax.rem(zero, 2)
    xl = lax.div(tp, 4)
    y = lax.rem(tp, 4)
    spot = lax.div(zero, 2)

    def tp_of(far, dy):
        other = lax.rem(xl + far, 2)
        return other * 4 + lax.rem(y + dy + 4, 4)

    def spot_of(far, dz):
        other = lax.rem(xh + far, 2)
        return lax.rem(z + dz + 4, 4) * 2 + other

    def tp_dev(far, dy):
        return (zero, tp_of(far, dy))

    def zero_dev(far, dz):
        return (spot_of(far, dz) * 2 + core, tp)

    sibling = (spot * 2 + (1 - core), tp)

    barrier = pltpu.get_barrier_semaphore()
    greeted = 0
    for k in range(1, 16):
        pl.semaphore_signal(barrier, inc=1, device_id=(lax.rem(zero + k, 16), tp), device_id_type=MESH)
        greeted += 1
    for k in range(1, 8):
        pl.semaphore_signal(barrier, inc=1, device_id=(zero, lax.rem(tp + k, 8)), device_id_type=MESH)
        greeted += 1
    diagonal = lax.broadcasted_iota(jnp.int32, (128, 128), 0) == lax.broadcasted_iota(jnp.int32, (128, 128), 1)
    own_rows = pl.ds(pl.multiple_of(core * 512, 512), 512)
    gains = gain[pl.ds(pl.multiple_of(zero * ROWS, ROWS), ROWS)].astype(F32).reshape(1, ROWS)
    for t in range(4):
        column = jnp.sum(jnp.where(diagonal, gains[:, t * 128:(t + 1) * 128], 0.0), axis=1, keepdims=True)
        here = pl.ds(pl.multiple_of(core * 512 + t * 128, 128), 128)
        there = pl.ds(t * 128, 128)
        wg[spot, here, 0:512] = (wq[there].astype(F32) * column).astype(BF16)
        wg[spot, here, 512:640] = (wk[there].astype(F32) * column).astype(BF16)
        wg[spot, here, 640:768] = (wv[there].astype(F32) * column).astype(BF16)

    pl.semaphore_wait(barrier, greeted)

    started = []

    def send(src, dst, send_sem, recv_sem, device):
        copy = pltpu.make_async_remote_copy(
            src_ref=src, dst_ref=dst, send_sem=send_sem, recv_sem=recv_sem, device_id=device, device_id_type=MESH
        )
        copy.start()
        started.append(copy)

    def arrived(ref, sem):
        pltpu.make_async_remote_copy(
            src_ref=ref, dst_ref=ref, send_sem=sem, recv_sem=sem, device_id=sibling, device_id_type=MESH
        ).wait_recv()

    class Gather:
        def __init__(self, block, index_of, device_of, pieces, send_sems, recv_sems, across_relay, copy_on):
            self.block, self.index_of, self.device_of, self.pieces = block, index_of, device_of, pieces
            self.send_sems, self.recv_sems = send_sems, recv_sems
            self.across_relay, self.copy_on = across_relay, copy_on
            self.count = 0

        def push(self, index, p, device, src=None):
            dst = self.block(index, p)
            send(dst if src is None else src, dst, self.send_sems.at[self.count], self.recv_sems.at[index, p], device)
            self.count += 1

        def wait(self, index, p):
            arrived(self.block(index, p), self.recv_sems.at[index, p])

        def on(self, index, p, src=None):
            if self.copy_on:
                self.push(index, p, sibling, src)

        def own(self, p, src=None):
            index = self.index_of(0, 0)
            self.push(index, p, self.device_of(1, 0), src)
            self.push(index, p, self.device_of(0, 1), src)
            self.push(index, p, self.device_of(0, -1), src)
            self.on(index, p, src)

        def across(self, p):
            index = self.index_of(1, 0)
            self.wait(index, p)
            self.push(index, p, self.device_of(0, 1))
            self.push(index, p, self.device_of(0, -1))
            self.on(index, p)

        def line(self, far, p):
            last = self.pieces - 1 - p
            below, above = self.index_of(far, -1), self.index_of(far, 1)
            relayed = (far == 0 or not self.across_relay) and p < self.pieces // 2
            self.wait(below, p)
            if relayed:
                self.push(below, p, self.device_of(0, 1))
            self.wait(above, last)
            if relayed:
                self.push(above, last, self.device_of(0, -1))
            self.on(below, p)
            self.on(above, last)

        def opposite(self, far, step):
            p = step // 2 if step % 2 == 0 else self.pieces - 1 - step // 2
            index = self.index_of(far, 2)
            self.wait(index, p)
            if far == 0 and self.across_relay:
                self.push(index, p, self.device_of(1, 0))
            self.on(index, p)

    def copied_on(gather):
        for far in range(2):
            for d in (0, 1, -1, 2):
                for p in range(gather.pieces):
                    gather.wait(spot_of(far, d) * 2 + (1 - core), p)

    h_rows = ROWS // H_PIECES
    hidden = Gather(
        lambda index, p: hg.at[index, pl.ds(p * h_rows, h_rows)], tp_of, tp_dev, H_PIECES, h_send, h_recv, True, False
    )
    w_rows = ROWS // W_PIECES
    weights = Gather(
        lambda index, p: wg.at[
            lax.div(index, 2), pl.ds(pl.multiple_of(lax.rem(index, 2) * 512 + p * w_rows, w_rows), w_rows)
        ],
        lambda far, dz: spot_of(far, dz) * 2 + core, zero_dev, W_PIECES, w_send, w_recv, False, True,
    )
    w_out = Gather(
        lambda index, p: wog.at[
            lax.rem(index, 2), pl.ds(p * 4, 4), pl.ds(pl.multiple_of(lax.div(index, 2) * 64, 64), 64)
        ],
        lambda far, dz: spot_of(far, dz) * 2 + core, zero_dev, 2, o_send, o_recv, False, True,
    )
    a_rows = ROWS // A_PIECES
    attended = Gather(
        lambda index, p: att.at[index, pl.ds(p * a_rows, a_rows)], tp_of, tp_dev, A_PIECES, a_send, a_recv, True, False
    )
    for p in range(4):
        hidden.own(p, hid.at[pl.ds(p * h_rows, h_rows)])
        weights.own(p)
    hg[tp] = hid[...]

    own = assignment[pl.ds(pl.multiple_of(zero * ROWS, ROWS), ROWS)].reshape(1, ROWS)
    row_id = lax.broadcasted_iota(jnp.int32, (ROWS, ROWS), 0)
    col_id = lax.broadcasted_iota(jnp.int32, (ROWS, ROWS), 1)
    equal = row_id == col_id
    own_col = jnp.sum(jnp.where(equal, own, 0), axis=1, keepdims=True)
    offset = jnp.sum(jnp.where((own == own_col) & (col_id < row_id), 1, 0), axis=1, keepdims=True)
    offset_row = jnp.sum(jnp.where(equal, offset, 0), axis=0, keepdims=True)
    runs[0:1, 0:ROWS] = own * CAP + offset_row
    runs[1:2, 0:ROWS] = own
    for k in range(16):
        blocks[k:k + 1, :] = assignment[pl.ds(k * ROWS, ROWS)].reshape(1, ROWS)
    counts = jnp.sum(jnp.where(blocks[...] == zero, 1, 0), axis=1, keepdims=True)
    row_16 = lax.broadcasted_iota(jnp.int32, (16, 16), 0)
    col_16 = lax.broadcasted_iota(jnp.int32, (16, 16), 1)
    counts_row = jnp.sum(jnp.where(row_16 == col_16, counts, 0), axis=0, keepdims=True)
    starts = jnp.sum(jnp.where(col_16 < row_16, counts_row, 0), axis=1, keepdims=True)
    slot = lax.broadcasted_iota(jnp.int32, (16, 16 * CAP), 1)
    place_in = slot - lax.broadcasted_iota(jnp.int32, (16, 16 * CAP), 0) * CAP
    filled = (place_in >= 0) & (place_in < CAP) & (place_in < counts)
    runs[2:3, :] = jnp.sum(jnp.where(filled, starts + place_in + 1, 0), axis=0, keepdims=True) - 1
    place_row = lax.broadcasted_iota(jnp.int32, (16, ROWS), 1)
    from_block = (place_row >= starts) & (place_row < starts + counts)
    runs[3:4, 0:ROWS] = jnp.sum(jnp.where(from_block, place_row - starts, 0), axis=0, keepdims=True)
    runs[4:5, 0:ROWS] = jnp.sum(
        jnp.where(from_block, lax.broadcasted_iota(jnp.int32, (16, ROWS), 0), 0), axis=0, keepdims=True
    )
    in_run = jnp.where(offset == lax.broadcasted_iota(jnp.int32, (ROWS, 64), 1), 1.0, 0.0)
    turns[:, 0:256] = jnp.dot(in_run, table[...], precision=lax.Precision.HIGHEST, preferred_element_type=F32)
    turns[:, 256:384] = jnp.broadcast_to(offset.astype(F32), (ROWS, 128))
    acc[...] = jnp.zeros_like(acc)
    lanes[...] = jnp.zeros_like(lanes)

    for p in range(2):
        hidden.line(0, p)
        weights.line(0, p)
    for p in range(4):
        hidden.across(p)
        hidden.opposite(0, p)
        weights.across(p)
    for p in range(2, 4):
        hidden.line(0, p)
        weights.line(0, p)
    for p in range(4):
        weights.line(1, p)
        weights.opposite(0, p)

    my_rows = pl.ds(pl.multiple_of(spot * 64, 64), 64)
    for k in range(1, 8):
        slot = lax.rem(spot + k, 8)
        rows = pl.ds(pl.multiple_of(slot * 64, 64), 64)
        send(wo.at[rows], dealt.at[spot], r_send.at[k], r_recv.at[k], (slot * 2 + core, tp))
    dealt[spot] = wo[my_rows]
    for p in range(4):
        weights.opposite(1, p)
    copied_on(weights)

    def project(index):
        block = hg[index]
        acc[...] += dot(block, wg[index])
        total = lanes[...]
        for c in range(8):
            wide = block[:, c * 128:(c + 1) * 128].astype(F32)
            total = total + wide * wide
        lanes[...] = total

    project(tp)
    project(tp_of(0, 1))
    project(tp_of(0, -1))
    for k in range(1, 8):
        arrived(dealt.at[lax.rem(spot + 8 - k, 8)], r_recv.at[k])
    for k in range(1, 8):
        to = lax.rem(tp + k, 8)
        send(dealt.at[to], wog.at[core, tp, my_rows], q_send.at[k], q_recv.at[k], (zero, to))
    wog[core, tp, my_rows] = dealt[tp]
    project(tp_of(0, 2))
    project(tp_of(1, 0))
    for p in range(4):
        hidden.line(1, p)
    project(tp_of(1, 1))
    project(tp_of(1, -1))
    for p in range(4):
        hidden.opposite(1, p)
    project(tp_of(1, 2))
    for k in range(1, 8):
        arrived(wog.at[core, lax.rem(tp + 8 - k, 8), my_rows], q_recv.at[k])
    for p in range(2):
        w_out.own(p)
    scale = lax.rsqrt(jnp.sum(lanes[...], axis=1, keepdims=True) * (1.0 / 8192) + EPSILON)
    cos, sin = turns[:, 0:128], turns[:, 128:256]
    for h in range(5):
        part = acc[:, h * HD:(h + 1) * HD] * scale
        qkv[:, h * HD:(h + 1) * HD] = (part * cos + pltpu.roll(part, 64, 1) * sin).astype(BF16)
    qkv[:, 640:768] = (acc[:, 640:768] * scale).astype(BF16)

    for t in range(4):
        first = max(t * 128 - 128, 0)
        keys = qkv[first:first + 256, 512:640]
        vals = qkv[first:first + 256, 640:768]
        row = lax.broadcasted_iota(jnp.int32, (128, 256), 0) + t * 128
        col = lax.broadcasted_iota(jnp.int32, (128, 256), 1) + first
        back = turns[t * 128:(t + 1) * 128, 256:384].astype(jnp.int32)
        allowed = (col <= row) & (col >= row - jnp.concatenate([back, back], axis=1))
        for h in range(4):
            query = qkv[t * 128:(t + 1) * 128, h * HD:(h + 1) * HD]
            scores = lax.dot_general(query, keys, (((1,), (1,)), ((), ())), preferred_element_type=F32)
            scores = jnp.where(allowed, scores * (HD ** -0.5), -1e30)
            weight = jnp.exp(scores - jnp.max(scores, axis=1, keepdims=True))
            probs = (weight / jnp.sum(weight, axis=1, keepdims=True)).astype(BF16)
            att[tp, t * 128:(t + 1) * 128, h * HD:(h + 1) * HD] = dot(probs, vals).astype(BF16)
        attended.own(t)

    w_out.line(0, 0)
    for p in range(2):
        attended.line(0, p)
    for p in range(2):
        attended.across(p)
        attended.opposite(0, p)
        w_out.across(p)
    for p in range(2, 4):
        attended.across(p)
        attended.opposite(0, p)
    w_out.line(0, 1)
    for p in range(2, 4):
        attended.line(0, p)
    for p in range(2):
        w_out.line(1, p)
        w_out.opposite(0, p)
    for step in range(2):
        w_out.opposite(1, step)
    copied_on(w_out)

    res[...] = hid[...].astype(F32)

    def output(index):
        for c in range(2):
            res[:, c * 512:(c + 1) * 512] += dot(att[index], wog[c, index])

    output(tp)
    output(tp_of(0, 1))
    output(tp_of(0, -1))
    output(tp_of(0, 2))
    output(tp_of(1, 0))
    for p in range(4):
        attended.line(1, p)
    output(tp_of(1, 1))
    output(tp_of(1, -1))
    for step in range(4):
        attended.opposite(1, step)
    output(tp_of(1, 2))

    def place(index):
        return pl.ds(pl.multiple_of(index * CAP, CAP), CAP)

    rounded = res[...].astype(BF16)
    for t in (2, 1, 3, 0):
        slots = lax.rem(lax.broadcasted_iota(jnp.int32, (256, ROWS), 0) + (zero * CAP + t * 256), 16 * CAP)
        chosen = jnp.where(slots == runs[0:1, 0:ROWS], 1.0, 0.0).astype(BF16)
        outgoing[t * 256:(t + 1) * 256, :] = dot(chosen, rounded).astype(BF16)
        for k in range(t * 4, t * 4 + 4):
            if k > 0:
                to = lax.rem(zero + k, 16)
                send(
                    outgoing.at[pl.ds(k * CAP, CAP)], incoming.at[place(zero)], x_send.at[k], x_recv.at[k], (to, tp)
                )
    incoming[place(zero)] = outgoing[0:CAP]

    squares = jnp.zeros((ROWS, 128), F32)
    along = jnp.zeros((ROWS, 128), F32)
    heads = head[pl.ds(pl.multiple_of(tp * FEATURES, FEATURES), FEATURES)].astype(F32).reshape(1, FEATURES)
    for c in range(8):
        part = res[:, c * 128:(c + 1) * 128]
        weight = heads[:, c * 128:(c + 1) * 128]
        squares = squares + part * part
        along = along + part * weight
    sums[tp, 0:1, :] = jnp.sum(squares.T, axis=0, keepdims=True)
    sums[tp, 1:2, :] = jnp.sum(along.T, axis=0, keepdims=True)
    for k in range(1, 8):
        send(sums.at[tp], sums.at[tp], v_send.at[k], v_recv.at[k], (zero, lax.rem(tp + k, 8)))
    for k in range(1, 8):
        arrived(sums.at[lax.rem(tp + 8 - k, 8)], v_recv.at[k])
    total = sums[0]
    for k in range(1, 8):
        total = total + sums[k]
    value = total[1:2] * lax.rsqrt(total[0:1] * (1.0 / 8192) + EPSILON)
    to_scorer = jnp.where(lax.broadcasted_iota(jnp.int32, (16, ROWS), 0) == runs[1:2, 0:ROWS], value, 0.0)
    back = turns[:, 256:384].astype(jnp.int32)
    in_place = jnp.where(back == lax.broadcasted_iota(jnp.int32, (ROWS, 128), 1), 1.0, 0.0)
    bucketed = jnp.dot(to_scorer, in_place, precision=lax.Precision.HIGHEST, preferred_element_type=F32)
    packed_values[...] = jnp.broadcast_to(bucketed[:, None, :], (16, 8, 128))
    for k in range(1, 16):
        to = lax.rem(zero + k, 16)
        send(packed_values.at[to], got_values.at[zero], y_send.at[k], y_recv.at[k], (to, tp))
    got_values[zero] = packed_values[zero]
    for k in range(1, 16):
        arrived(got_values.at[lax.rem(zero + 16 - k, 16)], y_recv.at[k])
    at_place = jnp.where(lax.broadcasted_iota(jnp.int32, (128, ROWS), 0) == runs[3:4, 0:ROWS], 1.0, 0.0)
    spread = jnp.dot(got_values[:, 0, :], at_place, precision=lax.Precision.HIGHEST, preferred_element_type=F32)
    mine = lax.broadcasted_iota(jnp.int32, (16, ROWS), 0) == runs[4:5, 0:ROWS]
    val_out[...] = jnp.sum(jnp.where(mine, spread, 0.0), axis=0, keepdims=True)

    for k in range(1, 16):
        arrived(incoming.at[place(lax.rem(zero + 16 - k, 16))], x_recv.at[k])
    for t in range(2):
        rows = lax.broadcasted_iota(jnp.int32, (256, 16 * CAP), 0) + t * 256
        chosen = jnp.where(rows == runs[2:3, :], 1.0, 0.0).astype(BF16)
        out[t * 256:(t + 1) * 256, :] = dot(chosen, incoming[...]).astype(BF16)
    for copy in started:
        copy.wait_send()


def rotary_table():
    angles = np.arange(CAP)[:, None] * ROPE_BASE ** (-2.0 * np.arange(HD // 2) / HD)[None, :]
    cosine, sine = np.cos(angles), np.sin(angles)
    return np.concatenate([cosine, cosine, -sine, sine], axis=1).astype(np.float32)


def shards(hidden_in, assignment, attn_gain, w_query, w_key, w_value_proj, w_out, value_head):
    vmem = pl.BlockSpec(memory_space=pltpu.VMEM)
    dma = pltpu.SemaphoreType.DMA
    scored, values = pl.pallas_call(
        layer,
        out_shape=(jax.ShapeDtypeStruct((ROWS, FEATURES), BF16), jax.ShapeDtypeStruct((1, ROWS), F32)),
        in_specs=[vmem] * 9,
        out_specs=(vmem, vmem),
        scratch_shapes=[
            pltpu.VMEM((8, ROWS, FEATURES), BF16),
            pltpu.VMEM((8, 2 * ROWS, QKV), BF16),
            pltpu.VMEM((2, 8, ROWS, 512), BF16),
            pltpu.VMEM((8, ROWS, 512), BF16),
            pltpu.VMEM((16 * CAP, FEATURES), BF16),
            pltpu.VMEM((16 * CAP, FEATURES), BF16),
            pltpu.VMEM((ROWS, QKV), F32),
            pltpu.VMEM((ROWS, QKV), BF16),
            pltpu.VMEM((ROWS, FEATURES), F32),
            pltpu.VMEM((8, 8, ROWS), F32),
            pltpu.VMEM((ROWS, 128), F32),
            pltpu.VMEM((16, ROWS), jnp.int32),
            pltpu.VMEM((ROWS, 384), F32),
            pltpu.VMEM((8, 16 * CAP), jnp.int32),
            pltpu.VMEM((16, 8, 128), F32),
            pltpu.VMEM((16, 8, 128), F32),
            pltpu.VMEM((8, 64, 512), BF16),
            dma((7 * H_PIECES,)), dma((8, H_PIECES)),
            dma((15 * W_PIECES,)), dma((16, W_PIECES)),
            dma((30,)), dma((16, 2)),
            dma((8,)), dma((8,)),
            dma((7 * A_PIECES,)), dma((8, A_PIECES)),
            dma((16,)), dma((16,)),
            dma((8,)), dma((8,)),
            dma((16,)), dma((16,)),
            dma((8,)), dma((8,)),
        ],
        compiler_params=pltpu.CompilerParams(
            collective_id=0, has_side_effects=True, vmem_limit_bytes=58 * 2**20
        ),
        name="layer",
    )(
        hidden_in, assignment, attn_gain, value_head, w_query, w_key, w_value_proj, w_out,
        jnp.asarray(rotary_table()),
    )
    return scored, values.reshape(ROWS)


def solution(mesh):
    in_specs = (P("zero", "tp"), P(), P(), P("zero", "tp"), P("zero", "tp"), P("zero", "tp"), P("tp", "zero"), P())
    return jax.shard_map(
        shards, mesh=mesh, in_specs=in_specs, out_specs=(P("zero", "tp"), P("zero")), check_vma=False
    )
```

```python
import jax
import jax.numpy as jnp
import numpy as np
from jax import lax
from jax.experimental import pallas as pl
from jax.experimental.pallas import tpu as pltpu
from jax.sharding import PartitionSpec as P

HD = 128
EPSILON = 1e-05
ROPE_BASE = 500000.0
MESH = pl.DeviceIdType.MESH
ROWS = 512
FEATURES = 1024
QKV = 768
CAP = 64
H_PIECES = 4
W_PIECES = 4
A_PIECES = 4
A_ENDS = 1
BF16 = jnp.bfloat16
F32 = jnp.float32


def dot(a, b):
    return jnp.dot(a, b, preferred_element_type=F32)


def layer(
    hid, assignment, gain, head, wq, wk, wv, wo, table,
    out, val_out,
    hg, wg, wog, att, outgoing, incoming, rounded, acc, qkv, res, sums, lanes, blocks, turns, runs, packed_values, got_values, dealt,
    h_send, h_recv, w_send, w_recv, o_send, o_recv, r_send, r_recv, a_send, a_recv,
    x_send, x_recv, v_send, v_recv, y_send, y_recv, q_send, q_recv,
):
    zero = lax.axis_index("zero")
    tp = lax.axis_index("tp")
    z = lax.div(zero, 4)
    xh = lax.rem(lax.div(zero, 2), 2)
    core = lax.rem(zero, 2)
    xl = lax.div(tp, 4)
    y = lax.rem(tp, 4)
    spot = lax.div(zero, 2)

    def tp_of(far, dy):
        other = lax.rem(xl + far, 2)
        return other * 4 + lax.rem(y + dy + 4, 4)

    def spot_of(far, dz):
        other = lax.rem(xh + far, 2)
        return lax.rem(z + dz + 4, 4) * 2 + other

    def tp_dev(far, dy):
        return (zero, tp_of(far, dy))

    def zero_dev(far, dz):
        return (spot_of(far, dz) * 2 + core, tp)

    sibling = (spot * 2 + (1 - core), tp)

    barrier = pltpu.get_barrier_semaphore()
    greeted = 0
    for k in range(1, 16):
        pl.semaphore_signal(barrier, inc=1, device_id=(lax.rem(zero + k, 16), tp), device_id_type=MESH)
        greeted += 1
    for k in range(1, 8):
        pl.semaphore_signal(barrier, inc=1, device_id=(zero, lax.rem(tp + k, 8)), device_id_type=MESH)
        greeted += 1
    diagonal = lax.broadcasted_iota(jnp.int32, (128, 128), 0) == lax.broadcasted_iota(jnp.int32, (128, 128), 1)
    own_rows = pl.ds(pl.multiple_of(core * 512, 512), 512)
    gains = gain[pl.ds(pl.multiple_of(zero * ROWS, ROWS), ROWS)].astype(F32).reshape(1, ROWS)
    for t in range(4):
        column = jnp.sum(jnp.where(diagonal, gains[:, t * 128:(t + 1) * 128], 0.0), axis=1, keepdims=True)
        here = pl.ds(pl.multiple_of(core * 512 + t * 128, 128), 128)
        there = pl.ds(t * 128, 128)
        wg[spot, here, 0:512] = (wq[there].astype(F32) * column).astype(BF16)
        wg[spot, here, 512:640] = (wk[there].astype(F32) * column).astype(BF16)
        wg[spot, here, 640:768] = (wv[there].astype(F32) * column).astype(BF16)

    pl.semaphore_wait(barrier, greeted)

    started = []

    def send(src, dst, send_sem, recv_sem, device):
        copy = pltpu.make_async_remote_copy(
            src_ref=src, dst_ref=dst, send_sem=send_sem, recv_sem=recv_sem, device_id=device, device_id_type=MESH
        )
        copy.start()
        started.append(copy)

    def arrived(ref, sem):
        pltpu.make_async_remote_copy(
            src_ref=ref, dst_ref=ref, send_sem=sem, recv_sem=sem, device_id=sibling, device_id_type=MESH
        ).wait_recv()

    class Gather:
        def __init__(self, block, index_of, device_of, pieces, send_sems, recv_sems, across_relay, copy_on, ends=0):
            self.block, self.index_of, self.device_of, self.pieces = block, index_of, device_of, pieces
            self.send_sems, self.recv_sems = send_sems, recv_sems
            self.across_relay, self.copy_on, self.ends = across_relay, copy_on, ends
            self.count = 0

        def push(self, index, p, device, src=None):
            dst = self.block(index, p)
            send(dst if src is None else src, dst, self.send_sems.at[self.count], self.recv_sems.at[index, p], device)
            self.count += 1

        def wait(self, index, p):
            arrived(self.block(index, p), self.recv_sems.at[index, p])

        def on(self, index, p, src=None):
            if self.copy_on:
                self.push(index, p, sibling, src)

        def own(self, p, src=None):
            index = self.index_of(0, 0)
            self.push(index, p, self.device_of(1, 0), src)
            self.push(index, p, self.device_of(0, 1), src)
            self.push(index, p, self.device_of(0, -1), src)
            self.on(index, p, src)

        def across(self, p):
            index = self.index_of(1, 0)
            self.wait(index, p)
            self.push(index, p, self.device_of(0, 1))
            self.push(index, p, self.device_of(0, -1))
            self.on(index, p)

        def line(self, far, p):
            last = self.pieces - 1 - p
            below, above = self.index_of(far, -1), self.index_of(far, 1)
            relayed = (far == 0 or not self.across_relay) and p < self.pieces // 2
            if far == 1 and self.across_relay:
                relayed = p < self.ends
            self.wait(below, p)
            if relayed:
                self.push(below, p, self.device_of(0, 1))
            self.wait(above, last)
            if relayed:
                self.push(above, last, self.device_of(0, -1))
            self.on(below, p)
            self.on(above, last)

        def opposite(self, far, step):
            p = step // 2 if step % 2 == 0 else self.pieces - 1 - step // 2
            index = self.index_of(far, 2)
            self.wait(index, p)
            if far == 0 and self.across_relay and self.ends <= p < self.pieces - self.ends:
                self.push(index, p, self.device_of(1, 0))
            self.on(index, p)

    def copied_on(gather, pieces):
        for far in range(2):
            for d in (0, 1, -1, 2):
                for p in pieces:
                    gather.wait(spot_of(far, d) * 2 + (1 - core), p)

    h_rows = ROWS // H_PIECES
    hidden = Gather(
        lambda index, p: hg.at[index, pl.ds(p * h_rows, h_rows)], tp_of, tp_dev, H_PIECES, h_send, h_recv, True, False
    )
    w_rows = ROWS // W_PIECES
    weights = Gather(
        lambda index, p: wg.at[
            lax.div(index, 2), pl.ds(pl.multiple_of(lax.rem(index, 2) * 512 + p * w_rows, w_rows), w_rows)
        ],
        lambda far, dz: spot_of(far, dz) * 2 + core, zero_dev, W_PIECES, w_send, w_recv, False, True,
    )
    w_out = Gather(
        lambda index, p: wog.at[
            lax.rem(index, 2), pl.ds(p // 2 * 4, 4), pl.ds(pl.multiple_of(lax.div(index, 2) * 64, 64), 64),
            pl.ds(0 if p in (0, 3) else 256, 256),
        ],
        lambda far, dz: spot_of(far, dz) * 2 + core, zero_dev, 4, o_send, o_recv, False, True,
    )
    a_rows = ROWS // A_PIECES
    attended = Gather(
        lambda index, p: att.at[index, pl.ds(p * a_rows, a_rows)], tp_of, tp_dev, A_PIECES, a_send, a_recv, True, False, A_ENDS
    )
    for p in range(4):
        hidden.own(p, hid.at[pl.ds(p * h_rows, h_rows)])
        weights.own(p)
    hg[tp] = hid[...]

    own = assignment[pl.ds(pl.multiple_of(zero * ROWS, ROWS), ROWS)].reshape(1, ROWS)
    row_id = lax.broadcasted_iota(jnp.int32, (ROWS, ROWS), 0)
    col_id = lax.broadcasted_iota(jnp.int32, (ROWS, ROWS), 1)
    equal = row_id == col_id
    own_col = jnp.sum(jnp.where(equal, own, 0), axis=1, keepdims=True)
    offset = jnp.sum(jnp.where((own == own_col) & (col_id < row_id), 1, 0), axis=1, keepdims=True)
    offset_row = jnp.sum(jnp.where(equal, offset, 0), axis=0, keepdims=True)
    runs[0:1, 0:ROWS] = own * CAP + offset_row
    runs[1:2, 0:ROWS] = own
    for k in range(16):
        blocks[k:k + 1, :] = assignment[pl.ds(k * ROWS, ROWS)].reshape(1, ROWS)
    counts = jnp.sum(jnp.where(blocks[...] == zero, 1, 0), axis=1, keepdims=True)
    row_16 = lax.broadcasted_iota(jnp.int32, (16, 16), 0)
    col_16 = lax.broadcasted_iota(jnp.int32, (16, 16), 1)
    counts_row = jnp.sum(jnp.where(row_16 == col_16, counts, 0), axis=0, keepdims=True)
    starts = jnp.sum(jnp.where(col_16 < row_16, counts_row, 0), axis=1, keepdims=True)
    slot = lax.broadcasted_iota(jnp.int32, (16, 16 * CAP), 1)
    place_in = slot - lax.broadcasted_iota(jnp.int32, (16, 16 * CAP), 0) * CAP
    filled = (place_in >= 0) & (place_in < CAP) & (place_in < counts)
    runs[2:3, :] = jnp.sum(jnp.where(filled, starts + place_in + 1, 0), axis=0, keepdims=True) - 1
    place_row = lax.broadcasted_iota(jnp.int32, (16, ROWS), 1)
    from_block = (place_row >= starts) & (place_row < starts + counts)
    runs[3:4, 0:ROWS] = jnp.sum(jnp.where(from_block, place_row - starts, 0), axis=0, keepdims=True)
    runs[4:5, 0:ROWS] = jnp.sum(
        jnp.where(from_block, lax.broadcasted_iota(jnp.int32, (16, ROWS), 0), 0), axis=0, keepdims=True
    )
    in_run = jnp.where(offset == lax.broadcasted_iota(jnp.int32, (ROWS, 64), 1), 1.0, 0.0)
    turns[:, 0:256] = jnp.dot(in_run, table[...], precision=lax.Precision.HIGHEST, preferred_element_type=F32)
    turns[:, 256:384] = jnp.broadcast_to(offset.astype(F32), (ROWS, 128))
    acc[...] = jnp.zeros_like(acc)
    lanes[...] = jnp.zeros_like(lanes)

    for p in range(2):
        hidden.line(0, p)
        weights.line(0, p)
    for p in range(4):
        hidden.across(p)
        hidden.opposite(0, p)
        weights.across(p)
    for p in range(2, 4):
        hidden.line(0, p)
        weights.line(0, p)
    for p in range(4):
        weights.line(1, p)
        weights.opposite(0, p)

    my_rows = pl.ds(pl.multiple_of(spot * 64, 64), 64)
    for k in range(1, 8):
        slot = lax.rem(spot + k, 8)
        rows = pl.ds(pl.multiple_of(slot * 64, 64), 64)
        send(wo.at[rows], dealt.at[spot], r_send.at[k], r_recv.at[k], (slot * 2 + core, tp))
    dealt[spot] = wo[my_rows]
    for p in range(4):
        weights.opposite(1, p)
    copied_on(weights, range(4))

    def project(index):
        block = hg[index]
        acc[...] += dot(block, wg[index])
        total = lanes[...]
        for c in range(8):
            wide = block[:, c * 128:(c + 1) * 128].astype(F32)
            total = total + wide * wide
        lanes[...] = total

    project(tp)
    project(tp_of(0, 1))
    project(tp_of(0, -1))
    for k in range(1, 8):
        arrived(dealt.at[lax.rem(spot + 8 - k, 8)], r_recv.at[k])
    for k in range(1, 8):
        to = lax.rem(tp + k, 8)
        send(dealt.at[to], wog.at[core, tp, my_rows], q_send.at[k], q_recv.at[k], (zero, to))
    wog[core, tp, my_rows] = dealt[tp]
    project(tp_of(0, 2))
    project(tp_of(1, 0))
    for p in range(4):
        hidden.line(1, p)
    project(tp_of(1, 1))
    project(tp_of(1, -1))
    for p in range(4):
        hidden.opposite(1, p)
    project(tp_of(1, 2))
    for k in range(1, 8):
        arrived(wog.at[core, lax.rem(tp + 8 - k, 8), my_rows], q_recv.at[k])
    for p in (0, 3, 1, 2):
        w_out.own(p)
    scale = lax.rsqrt(jnp.sum(lanes[...], axis=1, keepdims=True) * (1.0 / 8192) + EPSILON)
    cos, sin = turns[:, 0:128], turns[:, 128:256]
    for h in range(5):
        part = acc[:, h * HD:(h + 1) * HD] * scale
        qkv[:, h * HD:(h + 1) * HD] = (part * cos + pltpu.roll(part, 64, 1) * sin).astype(BF16)
    qkv[:, 640:768] = (acc[:, 640:768] * scale).astype(BF16)

    for t in range(4):
        first = max(t * 128 - 128, 0)
        keys = qkv[first:first + 256, 512:640]
        vals = qkv[first:first + 256, 640:768]
        row = lax.broadcasted_iota(jnp.int32, (128, 256), 0) + t * 128
        col = lax.broadcasted_iota(jnp.int32, (128, 256), 1) + first
        back = turns[t * 128:(t + 1) * 128, 256:384].astype(jnp.int32)
        allowed = (col <= row) & (col >= row - jnp.concatenate([back, back], axis=1))
        for h in range(4):
            query = qkv[t * 128:(t + 1) * 128, h * HD:(h + 1) * HD]
            scores = lax.dot_general(query, keys, (((1,), (1,)), ((), ())), preferred_element_type=F32)
            scores = jnp.where(allowed, scores * (HD ** -0.5), -1e30)
            weight = jnp.exp(scores - jnp.max(scores, axis=1, keepdims=True))
            probs = (weight / jnp.sum(weight, axis=1, keepdims=True)).astype(BF16)
            att[tp, t * 128:(t + 1) * 128, h * HD:(h + 1) * HD] = dot(probs, vals).astype(BF16)
        attended.own(t)

    w_out.line(0, 0)
    for p in range(2):
        attended.line(0, p)
    w_out.across(0)
    w_out.across(3)
    for p in range(2):
        attended.across(p)
        attended.opposite(0, p)
    w_out.line(1, 0)
    w_out.line(0, 1)
    for p in range(2, 4):
        attended.across(p)
        attended.opposite(0, p)
    w_out.across(1)
    w_out.across(2)
    for p in range(A_ENDS):
        attended.line(1, p)
    for p in range(2, 4):
        attended.line(0, p)
    w_out.line(1, 1)
    w_out.line(0, 3)
    w_out.line(1, 3)
    for step in range(2):
        w_out.opposite(0, step)
        w_out.opposite(1, step)
    copied_on(w_out, (0, 3))

    def output(h, index):
        for c in range(2):
            columns = pl.ds(c * 512 + h * 256, 256)
            res[:, columns] += dot(att[index], wog[c, index, :, h * 256:(h + 1) * 256])

    def place(index):
        return pl.ds(pl.multiple_of(index * CAP, CAP), CAP)

    def scatter(h):
        for c in range(2):
            rounded[:, c * 256:(c + 1) * 256] = res[:, c * 512 + h * 256:c * 512 + (h + 1) * 256].astype(BF16)
        for t in (2, 1, 3, 0):
            slots = lax.rem(lax.broadcasted_iota(jnp.int32, (256, ROWS), 0) + (zero * CAP + t * 256), 16 * CAP)
            chosen = jnp.where(slots == runs[0:1, 0:ROWS], 1.0, 0.0).astype(BF16)
            outgoing[h, t * 256:(t + 1) * 256, :] = dot(chosen, rounded[...]).astype(BF16)
            for k in range(t * 4, t * 4 + 4):
                if k > 0:
                    to = lax.rem(zero + k, 16)
                    send(
                        outgoing.at[h, pl.ds(k * CAP, CAP)], incoming.at[h, place(zero)],
                        x_send.at[h, k], x_recv.at[h, k], (to, tp),
                    )
        incoming[h, place(zero)] = outgoing[h, 0:CAP]

    res[...] = hid[...].astype(F32)
    output(0, tp)
    output(0, tp_of(0, 1))
    output(0, tp_of(0, -1))
    output(0, tp_of(0, 2))
    output(0, tp_of(1, 0))
    for p in range(A_ENDS, 4):
        attended.line(1, p)
    output(0, tp_of(1, 1))
    output(0, tp_of(1, -1))
    for step in range(4):
        attended.opposite(1, step)
    output(0, tp_of(1, 2))
    scatter(0)

    w_out.line(0, 2)
    w_out.line(1, 2)
    for step in range(2, 4):
        w_out.opposite(0, step)
        w_out.opposite(1, step)
    copied_on(w_out, (1, 2))
    for far, d in ((0, 0), (0, 1), (0, -1), (0, 2), (1, 0), (1, 1), (1, -1), (1, 2)):
        output(1, tp_of(far, d))

    squares = jnp.zeros((ROWS, 128), F32)
    along = jnp.zeros((ROWS, 128), F32)
    heads = head[pl.ds(pl.multiple_of(tp * FEATURES, FEATURES), FEATURES)].astype(F32).reshape(1, FEATURES)
    for c in range(8):
        part = res[:, c * 128:(c + 1) * 128]
        squares = squares + part * part
        along = along + part * heads[:, c * 128:(c + 1) * 128]
    sums[tp, 0:1, :] = jnp.sum(squares.T, axis=0, keepdims=True)
    sums[tp, 1:2, :] = jnp.sum(along.T, axis=0, keepdims=True)
    for k in range(1, 8):
        send(sums.at[tp], sums.at[tp], v_send.at[k], v_recv.at[k], (zero, lax.rem(tp + k, 8)))
    scatter(1)

    for k in range(1, 8):
        arrived(sums.at[lax.rem(tp + 8 - k, 8)], v_recv.at[k])
    total = sums[0]
    for k in range(1, 8):
        total = total + sums[k]
    value = total[1:2] * lax.rsqrt(total[0:1] * (1.0 / 8192) + EPSILON)
    to_scorer = jnp.where(lax.broadcasted_iota(jnp.int32, (16, ROWS), 0) == runs[1:2, 0:ROWS], value, 0.0)
    back = turns[:, 256:384].astype(jnp.int32)
    in_place = jnp.where(back == lax.broadcasted_iota(jnp.int32, (ROWS, 128), 1), 1.0, 0.0)
    bucketed = jnp.dot(to_scorer, in_place, precision=lax.Precision.HIGHEST, preferred_element_type=F32)
    packed_values[...] = jnp.broadcast_to(bucketed[:, None, :], (16, 8, 128))
    for k in range(1, 16):
        to = lax.rem(zero + k, 16)
        send(packed_values.at[to], got_values.at[zero], y_send.at[k], y_recv.at[k], (to, tp))
    got_values[zero] = packed_values[zero]
    for k in range(1, 16):
        arrived(got_values.at[lax.rem(zero + 16 - k, 16)], y_recv.at[k])
    at_place = jnp.where(lax.broadcasted_iota(jnp.int32, (128, ROWS), 0) == runs[3:4, 0:ROWS], 1.0, 0.0)
    spread = jnp.dot(got_values[:, 0, :], at_place, precision=lax.Precision.HIGHEST, preferred_element_type=F32)
    mine = lax.broadcasted_iota(jnp.int32, (16, ROWS), 0) == runs[4:5, 0:ROWS]
    val_out[...] = jnp.sum(jnp.where(mine, spread, 0.0), axis=0, keepdims=True)

    for h in range(2):
        for k in range(1, 16):
            arrived(incoming.at[h, place(lax.rem(zero + 16 - k, 16))], x_recv.at[h, k])
        for t in range(2):
            rows = lax.broadcasted_iota(jnp.int32, (256, 16 * CAP), 0) + t * 256
            chosen = jnp.where(rows == runs[2:3, :], 1.0, 0.0).astype(BF16)
            found = dot(chosen, incoming[h]).astype(BF16)
            for c in range(2):
                columns = pl.ds(c * 512 + h * 256, 256)
                out[t * 256:(t + 1) * 256, columns] = found[:, c * 256:(c + 1) * 256]
    for copy in started:
        copy.wait_send()


def rotary_table():
    angles = np.arange(CAP)[:, None] * ROPE_BASE ** (-2.0 * np.arange(HD // 2) / HD)[None, :]
    cosine, sine = np.cos(angles), np.sin(angles)
    return np.concatenate([cosine, cosine, -sine, sine], axis=1).astype(np.float32)


def shards(hidden_in, assignment, attn_gain, w_query, w_key, w_value_proj, w_out, value_head):
    vmem = pl.BlockSpec(memory_space=pltpu.VMEM)
    dma = pltpu.SemaphoreType.DMA
    scored, values = pl.pallas_call(
        layer,
        out_shape=(jax.ShapeDtypeStruct((ROWS, FEATURES), BF16), jax.ShapeDtypeStruct((1, ROWS), F32)),
        in_specs=[vmem] * 9,
        out_specs=(vmem, vmem),
        scratch_shapes=[
            pltpu.VMEM((8, ROWS, FEATURES), BF16),
            pltpu.VMEM((8, 2 * ROWS, QKV), BF16),
            pltpu.VMEM((2, 8, ROWS, 512), BF16),
            pltpu.VMEM((8, ROWS, 512), BF16),
            pltpu.VMEM((2, 16 * CAP, 512), BF16),
            pltpu.VMEM((2, 16 * CAP, 512), BF16),
            pltpu.VMEM((ROWS, 512), BF16),
            pltpu.VMEM((ROWS, QKV), F32),
            pltpu.VMEM((ROWS, QKV), BF16),
            pltpu.VMEM((ROWS, FEATURES), F32),
            pltpu.VMEM((8, 8, ROWS), F32),
            pltpu.VMEM((ROWS, 128), F32),
            pltpu.VMEM((16, ROWS), jnp.int32),
            pltpu.VMEM((ROWS, 384), F32),
            pltpu.VMEM((8, 16 * CAP), jnp.int32),
            pltpu.VMEM((16, 8, 128), F32),
            pltpu.VMEM((16, 8, 128), F32),
            pltpu.VMEM((8, 64, 512), BF16),
            dma((7 * H_PIECES,)), dma((8, H_PIECES)),
            dma((15 * W_PIECES,)), dma((16, W_PIECES)),
            dma((60,)), dma((16, 4)),
            dma((8,)), dma((8,)),
            dma((7 * A_PIECES,)), dma((8, A_PIECES)),
            dma((2, 16)), dma((2, 16)),
            dma((8,)), dma((8,)),
            dma((16,)), dma((16,)),
            dma((8,)), dma((8,)),
        ],
        compiler_params=pltpu.CompilerParams(
            collective_id=0, has_side_effects=True, vmem_limit_bytes=58 * 2**20
        ),
        name="layer",
    )(
        hidden_in, assignment, attn_gain, value_head, w_query, w_key, w_value_proj, w_out,
        jnp.asarray(rotary_table()),
    )
    return scored, values.reshape(ROWS)


def solution(mesh):
    in_specs = (P("zero", "tp"), P(), P(), P("zero", "tp"), P("zero", "tp"), P("zero", "tp"), P("tp", "zero"), P())
    return jax.shard_map(
        shards, mesh=mesh, in_specs=in_specs, out_specs=(P("zero", "tp"), P("zero")), check_vma=False
    )
```

```python
import jax
import jax.numpy as jnp
import numpy as np
from jax import lax
from jax.experimental import pallas as pl
from jax.experimental.pallas import tpu as pltpu
from jax.sharding import PartitionSpec as P

HD = 128
EPSILON = 1e-05
ROPE_BASE = 500000.0
MESH = pl.DeviceIdType.MESH
ROWS = 512
FEATURES = 1024
QKV = 768
CAP = 64
H_PIECES = 4
W_PIECES = 4
A_PIECES = 4
A_ENDS = 1
BF16 = jnp.bfloat16
F32 = jnp.float32


def dot(a, b):
    return jnp.dot(a, b, preferred_element_type=F32)


def layer(
    hid, assignment, gain, head, wq, wk, wv, wo, table,
    out, val_out,
    hg, wg, wog, att, outgoing, incoming, rounded, acc, qkv, res, sums, lanes, blocks, turns, runs, packed_values, got_values, dealt,
    h_send, h_recv, w_send, w_recv, o_send, o_recv, r_send, r_recv, a_send, a_recv,
    x_send, x_recv, v_send, v_recv, y_send, y_recv, q_send, q_recv,
):
    zero = lax.axis_index("zero")
    tp = lax.axis_index("tp")
    z = lax.div(zero, 4)
    xh = lax.rem(lax.div(zero, 2), 2)
    core = lax.rem(zero, 2)
    xl = lax.div(tp, 4)
    y = lax.rem(tp, 4)
    spot = lax.div(zero, 2)

    def tp_of(far, dy):
        other = lax.rem(xl + far, 2)
        return other * 4 + lax.rem(y + dy + 4, 4)

    def spot_of(far, dz):
        other = lax.rem(xh + far, 2)
        return lax.rem(z + dz + 4, 4) * 2 + other

    def tp_dev(far, dy):
        return (zero, tp_of(far, dy))

    def zero_dev(far, dz):
        return (spot_of(far, dz) * 2 + core, tp)

    sibling = (spot * 2 + (1 - core), tp)

    barrier = pltpu.get_barrier_semaphore()
    greeted = 0
    for k in range(1, 16):
        pl.semaphore_signal(barrier, inc=1, device_id=(lax.rem(zero + k, 16), tp), device_id_type=MESH)
        greeted += 1
    for k in range(1, 8):
        pl.semaphore_signal(barrier, inc=1, device_id=(zero, lax.rem(tp + k, 8)), device_id_type=MESH)
        greeted += 1
    diagonal = lax.broadcasted_iota(jnp.int32, (128, 128), 0) == lax.broadcasted_iota(jnp.int32, (128, 128), 1)
    own_rows = pl.ds(pl.multiple_of(core * 512, 512), 512)
    gains = gain[pl.ds(pl.multiple_of(zero * ROWS, ROWS), ROWS)].astype(F32).reshape(1, ROWS)
    for t in range(4):
        column = jnp.sum(jnp.where(diagonal, gains[:, t * 128:(t + 1) * 128], 0.0), axis=1, keepdims=True)
        here = pl.ds(pl.multiple_of(core * 512 + t * 128, 128), 128)
        there = pl.ds(t * 128, 128)
        wg[spot, here, 0:512] = (wq[there].astype(F32) * column).astype(BF16)
        wg[spot, here, 512:640] = (wk[there].astype(F32) * column).astype(BF16)
        wg[spot, here, 640:768] = (wv[there].astype(F32) * column).astype(BF16)

    pl.semaphore_wait(barrier, greeted)

    started = []

    def send(src, dst, send_sem, recv_sem, device):
        copy = pltpu.make_async_remote_copy(
            src_ref=src, dst_ref=dst, send_sem=send_sem, recv_sem=recv_sem, device_id=device, device_id_type=MESH
        )
        copy.start()
        started.append(copy)

    def arrived(ref, sem):
        pltpu.make_async_remote_copy(
            src_ref=ref, dst_ref=ref, send_sem=sem, recv_sem=sem, device_id=sibling, device_id_type=MESH
        ).wait_recv()

    class Gather:
        def __init__(self, block, index_of, device_of, pieces, send_sems, recv_sems, across_relay, copy_on, ends=0):
            self.block, self.index_of, self.device_of, self.pieces = block, index_of, device_of, pieces
            self.send_sems, self.recv_sems = send_sems, recv_sems
            self.across_relay, self.copy_on, self.ends = across_relay, copy_on, ends
            self.count = 0

        def push(self, index, p, device, src=None):
            dst = self.block(index, p)
            send(dst if src is None else src, dst, self.send_sems.at[self.count], self.recv_sems.at[index, p], device)
            self.count += 1

        def wait(self, index, p):
            arrived(self.block(index, p), self.recv_sems.at[index, p])

        def on(self, index, p, src=None):
            if self.copy_on:
                self.push(index, p, sibling, src)

        def own(self, p, src=None):
            index = self.index_of(0, 0)
            self.push(index, p, self.device_of(1, 0), src)
            self.push(index, p, self.device_of(0, 1), src)
            self.push(index, p, self.device_of(0, -1), src)
            self.on(index, p, src)

        def across(self, p):
            index = self.index_of(1, 0)
            self.wait(index, p)
            self.push(index, p, self.device_of(0, 1))
            self.push(index, p, self.device_of(0, -1))
            self.on(index, p)

        def line(self, far, p):
            last = self.pieces - 1 - p
            below, above = self.index_of(far, -1), self.index_of(far, 1)
            relayed = (far == 0 or not self.across_relay) and p < self.pieces // 2
            if far == 1 and self.across_relay:
                relayed = p < self.ends
            self.wait(below, p)
            if relayed:
                self.push(below, p, self.device_of(0, 1))
            self.wait(above, last)
            if relayed:
                self.push(above, last, self.device_of(0, -1))
            self.on(below, p)
            self.on(above, last)

        def opposite(self, far, step):
            p = step // 2 if step % 2 == 0 else self.pieces - 1 - step // 2
            index = self.index_of(far, 2)
            self.wait(index, p)
            if far == 0 and self.across_relay and self.ends <= p < self.pieces - self.ends:
                self.push(index, p, self.device_of(1, 0))
            self.on(index, p)

    def copied_on(gather, pieces):
        for far in range(2):
            for d in (0, 1, -1, 2):
                for p in pieces:
                    gather.wait(spot_of(far, d) * 2 + (1 - core), p)

    h_rows = ROWS // H_PIECES
    hidden = Gather(
        lambda index, p: hg.at[index, pl.ds(p * h_rows, h_rows)], tp_of, tp_dev, H_PIECES, h_send, h_recv, True, False
    )
    w_rows = ROWS // W_PIECES
    weights = Gather(
        lambda index, p: wg.at[
            lax.div(index, 2), pl.ds(pl.multiple_of(lax.rem(index, 2) * 512 + p * w_rows, w_rows), w_rows)
        ],
        lambda far, dz: spot_of(far, dz) * 2 + core, zero_dev, W_PIECES, w_send, w_recv, False, True,
    )
    w_out = Gather(
        lambda index, p: wog.at[
            lax.rem(index, 2), pl.ds(p // 2 * 4, 4), pl.ds(pl.multiple_of(lax.div(index, 2) * 64, 64), 64),
            pl.ds(0 if p in (0, 3) else 256, 256),
        ],
        lambda far, dz: spot_of(far, dz) * 2 + core, zero_dev, 4, o_send, o_recv, False, True,
    )
    a_rows = ROWS // A_PIECES
    attended = Gather(
        lambda index, p: att.at[index, pl.ds(p * a_rows, a_rows)], tp_of, tp_dev, A_PIECES, a_send, a_recv, True, False, A_ENDS
    )
    for p in range(4):
        hidden.own(p, hid.at[pl.ds(p * h_rows, h_rows)])
        weights.own(p)
    hg[tp] = hid[...]

    my_rows = pl.ds(pl.multiple_of(spot * 64, 64), 64)
    for k in range(1, 8):
        slot = lax.rem(spot + k, 8)
        rows = pl.ds(pl.multiple_of(slot * 64, 64), 64)
        send(wo.at[rows], dealt.at[spot], r_send.at[k], r_recv.at[k], (slot * 2 + core, tp))
    dealt[spot] = wo[my_rows]
    own = assignment[pl.ds(pl.multiple_of(zero * ROWS, ROWS), ROWS)].reshape(1, ROWS)
    row_id = lax.broadcasted_iota(jnp.int32, (ROWS, ROWS), 0)
    col_id = lax.broadcasted_iota(jnp.int32, (ROWS, ROWS), 1)
    equal = row_id == col_id
    own_col = jnp.sum(jnp.where(equal, own, 0), axis=1, keepdims=True)
    offset = jnp.sum(jnp.where((own == own_col) & (col_id < row_id), 1, 0), axis=1, keepdims=True)
    offset_row = jnp.sum(jnp.where(equal, offset, 0), axis=0, keepdims=True)
    runs[0:1, 0:ROWS] = own * CAP + offset_row
    runs[1:2, 0:ROWS] = own
    for k in range(16):
        blocks[k:k + 1, :] = assignment[pl.ds(k * ROWS, ROWS)].reshape(1, ROWS)
    counts = jnp.sum(jnp.where(blocks[...] == zero, 1, 0), axis=1, keepdims=True)
    row_16 = lax.broadcasted_iota(jnp.int32, (16, 16), 0)
    col_16 = lax.broadcasted_iota(jnp.int32, (16, 16), 1)
    counts_row = jnp.sum(jnp.where(row_16 == col_16, counts, 0), axis=0, keepdims=True)
    starts = jnp.sum(jnp.where(col_16 < row_16, counts_row, 0), axis=1, keepdims=True)
    slot = lax.broadcasted_iota(jnp.int32, (16, 16 * CAP), 1)
    place_in = slot - lax.broadcasted_iota(jnp.int32, (16, 16 * CAP), 0) * CAP
    filled = (place_in >= 0) & (place_in < CAP) & (place_in < counts)
    runs[2:3, :] = jnp.sum(jnp.where(filled, starts + place_in + 1, 0), axis=0, keepdims=True) - 1
    place_row = lax.broadcasted_iota(jnp.int32, (16, ROWS), 1)
    from_block = (place_row >= starts) & (place_row < starts + counts)
    runs[3:4, 0:ROWS] = jnp.sum(jnp.where(from_block, place_row - starts, 0), axis=0, keepdims=True)
    runs[4:5, 0:ROWS] = jnp.sum(
        jnp.where(from_block, lax.broadcasted_iota(jnp.int32, (16, ROWS), 0), 0), axis=0, keepdims=True
    )
    in_run = jnp.where(offset == lax.broadcasted_iota(jnp.int32, (ROWS, 64), 1), 1.0, 0.0)
    turns[:, 0:256] = jnp.dot(in_run, table[...], precision=lax.Precision.HIGHEST, preferred_element_type=F32)
    turns[:, 256:384] = jnp.broadcast_to(offset.astype(F32), (ROWS, 128))
    acc[...] = jnp.zeros_like(acc)
    lanes[...] = jnp.zeros_like(lanes)

    for p in range(2):
        hidden.line(0, p)
        weights.line(0, p)
    for p in range(4):
        hidden.across(p)
        hidden.opposite(0, p)
        weights.across(p)
    for p in range(2, 4):
        hidden.line(0, p)
        weights.line(0, p)
    for p in range(4):
        weights.line(1, p)
        weights.opposite(0, p)

    for p in range(4):
        weights.opposite(1, p)
    for k in range(1, 8):
        arrived(dealt.at[lax.rem(spot + 8 - k, 8)], r_recv.at[k])
    for k in range(1, 8):
        to = lax.rem(tp + k, 8)
        send(dealt.at[to], wog.at[core, tp, my_rows], q_send.at[k], q_recv.at[k], (zero, to))
    wog[core, tp, my_rows] = dealt[tp]
    copied_on(weights, range(4))

    def project(index):
        block = hg[index]
        acc[...] += dot(block, wg[index])
        total = lanes[...]
        for c in range(8):
            wide = block[:, c * 128:(c + 1) * 128].astype(F32)
            total = total + wide * wide
        lanes[...] = total

    project(tp)
    project(tp_of(0, 1))
    project(tp_of(0, -1))
    project(tp_of(0, 2))
    project(tp_of(1, 0))
    for p in range(4):
        hidden.line(1, p)
    project(tp_of(1, 1))
    project(tp_of(1, -1))
    for p in range(4):
        hidden.opposite(1, p)
    project(tp_of(1, 2))
    for k in range(1, 8):
        arrived(wog.at[core, lax.rem(tp + 8 - k, 8), my_rows], q_recv.at[k])
    for p in (0, 3, 1, 2):
        w_out.own(p)
    scale = lax.rsqrt(jnp.sum(lanes[...], axis=1, keepdims=True) * (1.0 / 8192) + EPSILON)
    cos, sin = turns[:, 0:128], turns[:, 128:256]
    for h in range(5):
        part = acc[:, h * HD:(h + 1) * HD] * scale
        qkv[:, h * HD:(h + 1) * HD] = (part * cos + pltpu.roll(part, 64, 1) * sin).astype(BF16)
    qkv[:, 640:768] = (acc[:, 640:768] * scale).astype(BF16)

    for t in range(4):
        first = max(t * 128 - 128, 0)
        keys = qkv[first:first + 256, 512:640]
        vals = qkv[first:first + 256, 640:768]
        row = lax.broadcasted_iota(jnp.int32, (128, 256), 0) + t * 128
        col = lax.broadcasted_iota(jnp.int32, (128, 256), 1) + first
        back = turns[t * 128:(t + 1) * 128, 256:384].astype(jnp.int32)
        allowed = (col <= row) & (col >= row - jnp.concatenate([back, back], axis=1))
        for h in range(4):
            query = qkv[t * 128:(t + 1) * 128, h * HD:(h + 1) * HD]
            scores = lax.dot_general(query, keys, (((1,), (1,)), ((), ())), preferred_element_type=F32)
            scores = jnp.where(allowed, scores * (HD ** -0.5), -1e30)
            weight = jnp.exp(scores - jnp.max(scores, axis=1, keepdims=True))
            probs = (weight / jnp.sum(weight, axis=1, keepdims=True)).astype(BF16)
            att[tp, t * 128:(t + 1) * 128, h * HD:(h + 1) * HD] = dot(probs, vals).astype(BF16)
        attended.own(t)

    w_out.line(0, 0)
    for p in range(2):
        attended.line(0, p)
    w_out.across(0)
    w_out.across(3)
    for p in range(2):
        attended.across(p)
        attended.opposite(0, p)
    w_out.line(1, 0)
    w_out.line(0, 1)
    for p in range(2, 4):
        attended.across(p)
        attended.opposite(0, p)
    w_out.across(1)
    w_out.across(2)
    for p in range(A_ENDS):
        attended.line(1, p)
    for p in range(2, 4):
        attended.line(0, p)
    w_out.line(1, 1)
    w_out.line(0, 3)
    w_out.line(1, 3)
    for step in range(2):
        w_out.opposite(0, step)
        w_out.opposite(1, step)
    copied_on(w_out, (0, 3))

    def output(h, index):
        for c in range(2):
            columns = pl.ds(c * 512 + h * 256, 256)
            res[:, columns] += dot(att[index], wog[c, index, :, h * 256:(h + 1) * 256])

    def place(index):
        return pl.ds(pl.multiple_of(index * CAP, CAP), CAP)

    def scatter(h):
        for c in range(2):
            rounded[:, c * 256:(c + 1) * 256] = res[:, c * 512 + h * 256:c * 512 + (h + 1) * 256].astype(BF16)
        for t in (2, 1, 3, 0):
            slots = lax.rem(lax.broadcasted_iota(jnp.int32, (256, ROWS), 0) + (zero * CAP + t * 256), 16 * CAP)
            chosen = jnp.where(slots == runs[0:1, 0:ROWS], 1.0, 0.0).astype(BF16)
            outgoing[h, t * 256:(t + 1) * 256, :] = dot(chosen, rounded[...]).astype(BF16)
            for k in range(t * 4, t * 4 + 4):
                if k > 0:
                    to = lax.rem(zero + k, 16)
                    send(
                        outgoing.at[h, pl.ds(k * CAP, CAP)], incoming.at[h, place(zero)],
                        x_send.at[h, k], x_recv.at[h, k], (to, tp),
                    )
        incoming[h, place(zero)] = outgoing[h, 0:CAP]

    res[...] = hid[...].astype(F32)
    output(0, tp)
    output(0, tp_of(0, 1))
    output(0, tp_of(0, -1))
    output(0, tp_of(0, 2))
    output(0, tp_of(1, 0))
    for p in range(A_ENDS, 4):
        attended.line(1, p)
    output(0, tp_of(1, 1))
    output(0, tp_of(1, -1))
    for step in range(4):
        attended.opposite(1, step)
    output(0, tp_of(1, 2))
    scatter(0)

    w_out.line(0, 2)
    w_out.line(1, 2)
    for step in range(2, 4):
        w_out.opposite(0, step)
        w_out.opposite(1, step)
    copied_on(w_out, (1, 2))
    for far, d in ((0, 0), (0, 1), (0, -1), (0, 2), (1, 0), (1, 1), (1, -1), (1, 2)):
        output(1, tp_of(far, d))

    squares = jnp.zeros((ROWS, 128), F32)
    along = jnp.zeros((ROWS, 128), F32)
    heads = head[pl.ds(pl.multiple_of(tp * FEATURES, FEATURES), FEATURES)].astype(F32).reshape(1, FEATURES)
    for c in range(8):
        part = res[:, c * 128:(c + 1) * 128]
        squares = squares + part * part
        along = along + part * heads[:, c * 128:(c + 1) * 128]
    sums[tp, 0:1, :] = jnp.sum(squares.T, axis=0, keepdims=True)
    sums[tp, 1:2, :] = jnp.sum(along.T, axis=0, keepdims=True)
    for k in range(1, 8):
        send(sums.at[tp], sums.at[tp], v_send.at[k], v_recv.at[k], (zero, lax.rem(tp + k, 8)))
    scatter(1)

    for k in range(1, 8):
        arrived(sums.at[lax.rem(tp + 8 - k, 8)], v_recv.at[k])
    total = sums[0]
    for k in range(1, 8):
        total = total + sums[k]
    value = total[1:2] * lax.rsqrt(total[0:1] * (1.0 / 8192) + EPSILON)
    to_scorer = jnp.where(lax.broadcasted_iota(jnp.int32, (16, ROWS), 0) == runs[1:2, 0:ROWS], value, 0.0)
    back = turns[:, 256:384].astype(jnp.int32)
    in_place = jnp.where(back == lax.broadcasted_iota(jnp.int32, (ROWS, 128), 1), 1.0, 0.0)
    bucketed = jnp.dot(to_scorer, in_place, precision=lax.Precision.HIGHEST, preferred_element_type=F32)
    packed_values[...] = jnp.broadcast_to(bucketed[:, None, :], (16, 8, 128))
    for k in range(1, 16):
        to = lax.rem(zero + k, 16)
        send(packed_values.at[to], got_values.at[zero], y_send.at[k], y_recv.at[k], (to, tp))
    got_values[zero] = packed_values[zero]
    for k in range(1, 16):
        arrived(got_values.at[lax.rem(zero + 16 - k, 16)], y_recv.at[k])
    at_place = jnp.where(lax.broadcasted_iota(jnp.int32, (128, ROWS), 0) == runs[3:4, 0:ROWS], 1.0, 0.0)
    spread = jnp.dot(got_values[:, 0, :], at_place, precision=lax.Precision.HIGHEST, preferred_element_type=F32)
    mine = lax.broadcasted_iota(jnp.int32, (16, ROWS), 0) == runs[4:5, 0:ROWS]
    val_out[...] = jnp.sum(jnp.where(mine, spread, 0.0), axis=0, keepdims=True)

    for h in range(2):
        for k in range(1, 16):
            arrived(incoming.at[h, place(lax.rem(zero + 16 - k, 16))], x_recv.at[h, k])
        for t in range(2):
            rows = lax.broadcasted_iota(jnp.int32, (256, 16 * CAP), 0) + t * 256
            chosen = jnp.where(rows == runs[2:3, :], 1.0, 0.0).astype(BF16)
            found = dot(chosen, incoming[h]).astype(BF16)
            for c in range(2):
                columns = pl.ds(c * 512 + h * 256, 256)
                out[t * 256:(t + 1) * 256, columns] = found[:, c * 256:(c + 1) * 256]
    for copy in started:
        copy.wait_send()


def rotary_table():
    angles = np.arange(CAP)[:, None] * ROPE_BASE ** (-2.0 * np.arange(HD // 2) / HD)[None, :]
    cosine, sine = np.cos(angles), np.sin(angles)
    return np.concatenate([cosine, cosine, -sine, sine], axis=1).astype(np.float32)


def shards(hidden_in, assignment, attn_gain, w_query, w_key, w_value_proj, w_out, value_head):
    vmem = pl.BlockSpec(memory_space=pltpu.VMEM)
    dma = pltpu.SemaphoreType.DMA
    scored, values = pl.pallas_call(
        layer,
        out_shape=(jax.ShapeDtypeStruct((ROWS, FEATURES), BF16), jax.ShapeDtypeStruct((1, ROWS), F32)),
        in_specs=[vmem] * 9,
        out_specs=(vmem, vmem),
        scratch_shapes=[
            pltpu.VMEM((8, ROWS, FEATURES), BF16),
            pltpu.VMEM((8, 2 * ROWS, QKV), BF16),
            pltpu.VMEM((2, 8, ROWS, 512), BF16),
            pltpu.VMEM((8, ROWS, 512), BF16),
            pltpu.VMEM((2, 16 * CAP, 512), BF16),
            pltpu.VMEM((2, 16 * CAP, 512), BF16),
            pltpu.VMEM((ROWS, 512), BF16),
            pltpu.VMEM((ROWS, QKV), F32),
            pltpu.VMEM((ROWS, QKV), BF16),
            pltpu.VMEM((ROWS, FEATURES), F32),
            pltpu.VMEM((8, 8, ROWS), F32),
            pltpu.VMEM((ROWS, 128), F32),
            pltpu.VMEM((16, ROWS), jnp.int32),
            pltpu.VMEM((ROWS, 384), F32),
            pltpu.VMEM((8, 16 * CAP), jnp.int32),
            pltpu.VMEM((16, 8, 128), F32),
            pltpu.VMEM((16, 8, 128), F32),
            pltpu.VMEM((8, 64, 512), BF16),
            dma((7 * H_PIECES,)), dma((8, H_PIECES)),
            dma((15 * W_PIECES,)), dma((16, W_PIECES)),
            dma((60,)), dma((16, 4)),
            dma((8,)), dma((8,)),
            dma((7 * A_PIECES,)), dma((8, A_PIECES)),
            dma((2, 16)), dma((2, 16)),
            dma((8,)), dma((8,)),
            dma((16,)), dma((16,)),
            dma((8,)), dma((8,)),
        ],
        compiler_params=pltpu.CompilerParams(
            collective_id=0, has_side_effects=True, vmem_limit_bytes=58 * 2**20
        ),
        name="layer",
    )(
        hidden_in, assignment, attn_gain, value_head, w_query, w_key, w_value_proj, w_out,
        jnp.asarray(rotary_table()),
    )
    return scored, values.reshape(ROWS)


def solution(mesh):
    in_specs = (P("zero", "tp"), P(), P(), P("zero", "tp"), P("zero", "tp"), P("zero", "tp"), P("tp", "zero"), P())
    return jax.shard_map(
        shards, mesh=mesh, in_specs=in_specs, out_specs=(P("zero", "tp"), P("zero")), check_vma=False
    )
```

```python
import jax
import jax.numpy as jnp
import numpy as np
from jax import lax
from jax.experimental import pallas as pl
from jax.experimental.pallas import tpu as pltpu
from jax.sharding import PartitionSpec as P

HD = 128
EPSILON = 1e-05
ROPE_BASE = 500000.0
MESH = pl.DeviceIdType.MESH
ROWS = 512
FEATURES = 1024
QKV = 768
CAP = 64
H_PIECES = 4
W_PIECES = 4
A_PIECES = 4
A_ENDS = 1
BF16 = jnp.bfloat16
F32 = jnp.float32


def dot(a, b):
    return jnp.dot(a, b, preferred_element_type=F32)


def layer(
    hid, assignment, gain, head, wq, wk, wv, wo, table,
    out, val_out,
    hg, wg, wog, att, outgoing, incoming, rounded, acc, qkv, res, sums, lanes, blocks, turns, runs, packed_values, got_values, dealt,
    h_send, h_recv, w_send, w_recv, o_send, o_recv, r_send, r_recv, a_send, a_recv,
    x_send, x_recv, v_send, v_recv, y_send, y_recv, q_send, q_recv,
):
    zero = lax.axis_index("zero")
    tp = lax.axis_index("tp")
    z = lax.div(zero, 4)
    xh = lax.rem(lax.div(zero, 2), 2)
    core = lax.rem(zero, 2)
    xl = lax.div(tp, 4)
    y = lax.rem(tp, 4)
    spot = lax.div(zero, 2)

    def tp_of(far, dy):
        other = lax.rem(xl + far, 2)
        return other * 4 + lax.rem(y + dy + 4, 4)

    def spot_of(far, dz):
        other = lax.rem(xh + far, 2)
        return lax.rem(z + dz + 4, 4) * 2 + other

    def tp_dev(far, dy):
        return (zero, tp_of(far, dy))

    def zero_dev(far, dz):
        return (spot_of(far, dz) * 2 + core, tp)

    sibling = (spot * 2 + (1 - core), tp)

    barrier = pltpu.get_barrier_semaphore()
    greeted = 0
    for k in range(1, 16):
        pl.semaphore_signal(barrier, inc=1, device_id=(lax.rem(zero + k, 16), tp), device_id_type=MESH)
        greeted += 1
    for k in range(1, 8):
        pl.semaphore_signal(barrier, inc=1, device_id=(zero, lax.rem(tp + k, 8)), device_id_type=MESH)
        greeted += 1
    diagonal = lax.broadcasted_iota(jnp.int32, (128, 128), 0) == lax.broadcasted_iota(jnp.int32, (128, 128), 1)
    own_rows = pl.ds(pl.multiple_of(core * 512, 512), 512)
    gains = gain[pl.ds(pl.multiple_of(zero * ROWS, ROWS), ROWS)].astype(F32).reshape(1, ROWS)
    for t in range(4):
        column = jnp.sum(jnp.where(diagonal, gains[:, t * 128:(t + 1) * 128], 0.0), axis=1, keepdims=True)
        here = pl.ds(pl.multiple_of(core * 512 + t * 128, 128), 128)
        there = pl.ds(t * 128, 128)
        wg[spot, here, 0:512] = (wq[there].astype(F32) * column).astype(BF16)
        wg[spot, here, 512:640] = (wk[there].astype(F32) * column).astype(BF16)
        wg[spot, here, 640:768] = (wv[there].astype(F32) * column).astype(BF16)

    pl.semaphore_wait(barrier, greeted)

    started = []

    def send(src, dst, send_sem, recv_sem, device):
        copy = pltpu.make_async_remote_copy(
            src_ref=src, dst_ref=dst, send_sem=send_sem, recv_sem=recv_sem, device_id=device, device_id_type=MESH
        )
        copy.start()
        started.append(copy)

    def arrived(ref, sem):
        pltpu.make_async_remote_copy(
            src_ref=ref, dst_ref=ref, send_sem=sem, recv_sem=sem, device_id=sibling, device_id_type=MESH
        ).wait_recv()

    class Gather:
        def __init__(self, block, index_of, device_of, pieces, send_sems, recv_sems, across_relay, copy_on, ends=0):
            self.block, self.index_of, self.device_of, self.pieces = block, index_of, device_of, pieces
            self.send_sems, self.recv_sems = send_sems, recv_sems
            self.across_relay, self.copy_on, self.ends = across_relay, copy_on, ends
            self.count = 0

        def push(self, index, p, device, src=None):
            dst = self.block(index, p)
            send(dst if src is None else src, dst, self.send_sems.at[self.count], self.recv_sems.at[index, p], device)
            self.count += 1

        def wait(self, index, p):
            arrived(self.block(index, p), self.recv_sems.at[index, p])

        def on(self, index, p, src=None):
            if self.copy_on:
                self.push(index, p, sibling, src)

        def own(self, p, src=None):
            index = self.index_of(0, 0)
            self.push(index, p, self.device_of(1, 0), src)
            self.push(index, p, self.device_of(0, 1), src)
            self.push(index, p, self.device_of(0, -1), src)
            self.on(index, p, src)

        def across(self, p):
            index = self.index_of(1, 0)
            self.wait(index, p)
            self.push(index, p, self.device_of(0, 1))
            self.push(index, p, self.device_of(0, -1))
            self.on(index, p)

        def line(self, far, p):
            last = self.pieces - 1 - p
            below, above = self.index_of(far, -1), self.index_of(far, 1)
            relayed = (far == 0 or not self.across_relay) and p < self.pieces // 2
            if far == 1 and self.across_relay:
                relayed = p < self.ends
            self.wait(below, p)
            if relayed:
                self.push(below, p, self.device_of(0, 1))
            self.wait(above, last)
            if relayed:
                self.push(above, last, self.device_of(0, -1))
            self.on(below, p)
            self.on(above, last)

        def opposite(self, far, step):
            p = step // 2 if step % 2 == 0 else self.pieces - 1 - step // 2
            index = self.index_of(far, 2)
            self.wait(index, p)
            if far == 0 and self.across_relay and self.ends <= p < self.pieces - self.ends:
                self.push(index, p, self.device_of(1, 0))
            self.on(index, p)

    def copied_on(gather, pieces):
        for far in range(2):
            for d in (0, 1, -1, 2):
                for p in pieces:
                    gather.wait(spot_of(far, d) * 2 + (1 - core), p)

    h_rows = ROWS // H_PIECES
    hidden = Gather(
        lambda index, p: hg.at[index, pl.ds(p * h_rows, h_rows)], tp_of, tp_dev, H_PIECES, h_send, h_recv, True, False
    )
    w_rows = ROWS // W_PIECES
    weights = Gather(
        lambda index, p: wg.at[
            lax.div(index, 2), pl.ds(pl.multiple_of(lax.rem(index, 2) * 512 + p * w_rows, w_rows), w_rows)
        ],
        lambda far, dz: spot_of(far, dz) * 2 + core, zero_dev, W_PIECES, w_send, w_recv, False, True,
    )
    w_out = Gather(
        lambda index, p: wog.at[
            lax.rem(index, 2), pl.ds(p // 2 * 4, 4), pl.ds(pl.multiple_of(lax.div(index, 2) * 64, 64), 64),
            pl.ds(0 if p in (0, 3) else 256, 256),
        ],
        lambda far, dz: spot_of(far, dz) * 2 + core, zero_dev, 4, o_send, o_recv, True, True, 1,
    )
    a_rows = ROWS // A_PIECES
    attended = Gather(
        lambda index, p: att.at[index, pl.ds(p * a_rows, a_rows)], tp_of, tp_dev, A_PIECES, a_send, a_recv, True, False, A_ENDS
    )
    for p in range(4):
        hidden.own(p, hid.at[pl.ds(p * h_rows, h_rows)])
        weights.own(p)
    hg[tp] = hid[...]

    my_rows = pl.ds(pl.multiple_of(spot * 64, 64), 64)
    for k in range(1, 8):
        slot = lax.rem(spot + k, 8)
        rows = pl.ds(pl.multiple_of(slot * 64, 64), 64)
        send(wo.at[rows], dealt.at[spot], r_send.at[k], r_recv.at[k], (slot * 2 + core, tp))
    dealt[spot] = wo[my_rows]
    own = assignment[pl.ds(pl.multiple_of(zero * ROWS, ROWS), ROWS)].reshape(1, ROWS)
    row_id = lax.broadcasted_iota(jnp.int32, (ROWS, ROWS), 0)
    col_id = lax.broadcasted_iota(jnp.int32, (ROWS, ROWS), 1)
    equal = row_id == col_id
    own_col = jnp.sum(jnp.where(equal, own, 0), axis=1, keepdims=True)
    offset = jnp.sum(jnp.where((own == own_col) & (col_id < row_id), 1, 0), axis=1, keepdims=True)
    offset_row = jnp.sum(jnp.where(equal, offset, 0), axis=0, keepdims=True)
    runs[0:1, 0:ROWS] = own * CAP + offset_row
    runs[1:2, 0:ROWS] = own
    for k in range(16):
        blocks[k:k + 1, :] = assignment[pl.ds(k * ROWS, ROWS)].reshape(1, ROWS)
    counts = jnp.sum(jnp.where(blocks[...] == zero, 1, 0), axis=1, keepdims=True)
    row_16 = lax.broadcasted_iota(jnp.int32, (16, 16), 0)
    col_16 = lax.broadcasted_iota(jnp.int32, (16, 16), 1)
    counts_row = jnp.sum(jnp.where(row_16 == col_16, counts, 0), axis=0, keepdims=True)
    starts = jnp.sum(jnp.where(col_16 < row_16, counts_row, 0), axis=1, keepdims=True)
    slot = lax.broadcasted_iota(jnp.int32, (16, 16 * CAP), 1)
    place_in = slot - lax.broadcasted_iota(jnp.int32, (16, 16 * CAP), 0) * CAP
    filled = (place_in >= 0) & (place_in < CAP) & (place_in < counts)
    runs[2:3, :] = jnp.sum(jnp.where(filled, starts + place_in + 1, 0), axis=0, keepdims=True) - 1
    place_row = lax.broadcasted_iota(jnp.int32, (16, ROWS), 1)
    from_block = (place_row >= starts) & (place_row < starts + counts)
    runs[3:4, 0:ROWS] = jnp.sum(jnp.where(from_block, place_row - starts, 0), axis=0, keepdims=True)
    runs[4:5, 0:ROWS] = jnp.sum(
        jnp.where(from_block, lax.broadcasted_iota(jnp.int32, (16, ROWS), 0), 0), axis=0, keepdims=True
    )
    in_run = jnp.where(offset == lax.broadcasted_iota(jnp.int32, (ROWS, 64), 1), 1.0, 0.0)
    turns[:, 0:256] = jnp.dot(in_run, table[...], precision=lax.Precision.HIGHEST, preferred_element_type=F32)
    turns[:, 256:384] = jnp.broadcast_to(offset.astype(F32), (ROWS, 128))
    acc[...] = jnp.zeros_like(acc)
    lanes[...] = jnp.zeros_like(lanes)

    for p in range(2):
        hidden.line(0, p)
        weights.line(0, p)
    for p in range(4):
        hidden.across(p)
        hidden.opposite(0, p)
        weights.across(p)
    for p in range(2, 4):
        hidden.line(0, p)
        weights.line(0, p)
    for p in range(4):
        weights.line(1, p)
        weights.opposite(0, p)

    for p in range(4):
        weights.opposite(1, p)
    for k in range(1, 8):
        arrived(dealt.at[lax.rem(spot + 8 - k, 8)], r_recv.at[k])
    for k in range(1, 8):
        to = lax.rem(tp + k, 8)
        send(dealt.at[to], wog.at[core, tp, my_rows], q_send.at[k], q_recv.at[k], (zero, to))
    wog[core, tp, my_rows] = dealt[tp]
    copied_on(weights, range(4))

    def project(index):
        block = hg[index]
        acc[...] += dot(block, wg[index])
        total = lanes[...]
        for c in range(8):
            wide = block[:, c * 128:(c + 1) * 128].astype(F32)
            total = total + wide * wide
        lanes[...] = total

    project(tp)
    project(tp_of(0, 1))
    project(tp_of(0, -1))
    project(tp_of(0, 2))
    project(tp_of(1, 0))
    for p in range(4):
        hidden.line(1, p)
    project(tp_of(1, 1))
    project(tp_of(1, -1))
    for p in range(4):
        hidden.opposite(1, p)
    project(tp_of(1, 2))
    for k in range(1, 8):
        arrived(wog.at[core, lax.rem(tp + 8 - k, 8), my_rows], q_recv.at[k])
    for p in (0, 3, 1, 2):
        w_out.own(p)
    scale = lax.rsqrt(jnp.sum(lanes[...], axis=1, keepdims=True) * (1.0 / 8192) + EPSILON)
    cos, sin = turns[:, 0:128], turns[:, 128:256]
    for h in range(5):
        part = acc[:, h * HD:(h + 1) * HD] * scale
        qkv[:, h * HD:(h + 1) * HD] = (part * cos + pltpu.roll(part, 64, 1) * sin).astype(BF16)
    qkv[:, 640:768] = (acc[:, 640:768] * scale).astype(BF16)

    for t in range(4):
        first = max(t * 128 - 128, 0)
        keys = qkv[first:first + 256, 512:640]
        vals = qkv[first:first + 256, 640:768]
        row = lax.broadcasted_iota(jnp.int32, (128, 256), 0) + t * 128
        col = lax.broadcasted_iota(jnp.int32, (128, 256), 1) + first
        back = turns[t * 128:(t + 1) * 128, 256:384].astype(jnp.int32)
        allowed = (col <= row) & (col >= row - jnp.concatenate([back, back], axis=1))
        for h in range(4):
            query = qkv[t * 128:(t + 1) * 128, h * HD:(h + 1) * HD]
            scores = lax.dot_general(query, keys, (((1,), (1,)), ((), ())), preferred_element_type=F32)
            scores = jnp.where(allowed, scores * (HD ** -0.5), -1e30)
            weight = jnp.exp(scores - jnp.max(scores, axis=1, keepdims=True))
            probs = (weight / jnp.sum(weight, axis=1, keepdims=True)).astype(BF16)
            att[tp, t * 128:(t + 1) * 128, h * HD:(h + 1) * HD] = dot(probs, vals).astype(BF16)
        attended.own(t)

    w_out.line(0, 0)
    for p in range(2):
        attended.line(0, p)
    w_out.across(0)
    w_out.across(3)
    for p in range(2):
        attended.across(p)
        attended.opposite(0, p)
    w_out.line(1, 0)
    w_out.line(0, 1)
    for p in range(2, 4):
        attended.across(p)
        attended.opposite(0, p)
    w_out.across(1)
    w_out.across(2)
    for p in range(A_ENDS):
        attended.line(1, p)
    for p in range(2, 4):
        attended.line(0, p)
    w_out.line(1, 1)
    w_out.line(0, 3)
    w_out.line(1, 3)
    for step in range(2):
        w_out.opposite(0, step)
        w_out.opposite(1, step)
    copied_on(w_out, (0, 3))

    def output(h, index):
        for c in range(2):
            columns = pl.ds(c * 512 + h * 256, 256)
            res[:, columns] += dot(att[index], wog[c, index, :, h * 256:(h + 1) * 256])

    def place(index):
        return pl.ds(pl.multiple_of(index * CAP, CAP), CAP)

    def scatter(h):
        for c in range(2):
            rounded[:, c * 256:(c + 1) * 256] = res[:, c * 512 + h * 256:c * 512 + (h + 1) * 256].astype(BF16)
        for t in (2, 1, 3, 0):
            slots = lax.rem(lax.broadcasted_iota(jnp.int32, (256, ROWS), 0) + (zero * CAP + t * 256), 16 * CAP)
            chosen = jnp.where(slots == runs[0:1, 0:ROWS], 1.0, 0.0).astype(BF16)
            outgoing[h, t * 256:(t + 1) * 256, :] = dot(chosen, rounded[...]).astype(BF16)
            for k in range(t * 4, t * 4 + 4):
                if k > 0:
                    to = lax.rem(zero + k, 16)
                    send(
                        outgoing.at[h, pl.ds(k * CAP, CAP)], incoming.at[h, place(zero)],
                        x_send.at[h, k], x_recv.at[h, k], (to, tp),
                    )
        incoming[h, place(zero)] = outgoing[h, 0:CAP]

    res[...] = hid[...].astype(F32)
    output(0, tp)
    output(0, tp_of(0, 1))
    output(0, tp_of(0, -1))
    output(0, tp_of(0, 2))
    output(0, tp_of(1, 0))
    for step in range(2, 4):
        w_out.opposite(0, step)
    for p in range(A_ENDS, 4):
        attended.line(1, p)
    output(0, tp_of(1, 1))
    output(0, tp_of(1, -1))
    for step in range(4):
        attended.opposite(1, step)
    output(0, tp_of(1, 2))
    scatter(0)

    w_out.line(0, 2)
    w_out.line(1, 2)
    for step in range(2, 4):
        w_out.opposite(1, step)
    copied_on(w_out, (1, 2))
    for far, d in ((0, 0), (0, 1), (0, -1), (0, 2), (1, 0), (1, 1), (1, -1), (1, 2)):
        output(1, tp_of(far, d))

    squares = jnp.zeros((ROWS, 128), F32)
    along = jnp.zeros((ROWS, 128), F32)
    heads = head[pl.ds(pl.multiple_of(tp * FEATURES, FEATURES), FEATURES)].astype(F32).reshape(1, FEATURES)
    for c in range(8):
        part = res[:, c * 128:(c + 1) * 128]
        squares = squares + part * part
        along = along + part * heads[:, c * 128:(c + 1) * 128]
    sums[tp, 0:1, :] = jnp.sum(squares.T, axis=0, keepdims=True)
    sums[tp, 1:2, :] = jnp.sum(along.T, axis=0, keepdims=True)
    for k in range(1, 8):
        send(sums.at[tp], sums.at[tp], v_send.at[k], v_recv.at[k], (zero, lax.rem(tp + k, 8)))
    scatter(1)

    for k in range(1, 8):
        arrived(sums.at[lax.rem(tp + 8 - k, 8)], v_recv.at[k])
    total = sums[0]
    for k in range(1, 8):
        total = total + sums[k]
    value = total[1:2] * lax.rsqrt(total[0:1] * (1.0 / 8192) + EPSILON)
    to_scorer = jnp.where(lax.broadcasted_iota(jnp.int32, (16, ROWS), 0) == runs[1:2, 0:ROWS], value, 0.0)
    back = turns[:, 256:384].astype(jnp.int32)
    in_place = jnp.where(back == lax.broadcasted_iota(jnp.int32, (ROWS, 128), 1), 1.0, 0.0)
    bucketed = jnp.dot(to_scorer, in_place, precision=lax.Precision.HIGHEST, preferred_element_type=F32)
    packed_values[...] = jnp.broadcast_to(bucketed[:, None, :], (16, 8, 128))
    for k in range(1, 16):
        to = lax.rem(zero + k, 16)
        send(packed_values.at[to], got_values.at[zero], y_send.at[k], y_recv.at[k], (to, tp))
    got_values[zero] = packed_values[zero]
    for k in range(1, 16):
        arrived(got_values.at[lax.rem(zero + 16 - k, 16)], y_recv.at[k])
    at_place = jnp.where(lax.broadcasted_iota(jnp.int32, (128, ROWS), 0) == runs[3:4, 0:ROWS], 1.0, 0.0)
    spread = jnp.dot(got_values[:, 0, :], at_place, precision=lax.Precision.HIGHEST, preferred_element_type=F32)
    mine = lax.broadcasted_iota(jnp.int32, (16, ROWS), 0) == runs[4:5, 0:ROWS]
    val_out[...] = jnp.sum(jnp.where(mine, spread, 0.0), axis=0, keepdims=True)

    for h in range(2):
        for k in range(1, 16):
            arrived(incoming.at[h, place(lax.rem(zero + 16 - k, 16))], x_recv.at[h, k])
        for t in range(2):
            rows = lax.broadcasted_iota(jnp.int32, (256, 16 * CAP), 0) + t * 256
            chosen = jnp.where(rows == runs[2:3, :], 1.0, 0.0).astype(BF16)
            found = dot(chosen, incoming[h]).astype(BF16)
            for c in range(2):
                columns = pl.ds(c * 512 + h * 256, 256)
                out[t * 256:(t + 1) * 256, columns] = found[:, c * 256:(c + 1) * 256]
    for copy in started:
        copy.wait_send()


def rotary_table():
    angles = np.arange(CAP)[:, None] * ROPE_BASE ** (-2.0 * np.arange(HD // 2) / HD)[None, :]
    cosine, sine = np.cos(angles), np.sin(angles)
    return np.concatenate([cosine, cosine, -sine, sine], axis=1).astype(np.float32)


def shards(hidden_in, assignment, attn_gain, w_query, w_key, w_value_proj, w_out, value_head):
    vmem = pl.BlockSpec(memory_space=pltpu.VMEM)
    dma = pltpu.SemaphoreType.DMA
    scored, values = pl.pallas_call(
        layer,
        out_shape=(jax.ShapeDtypeStruct((ROWS, FEATURES), BF16), jax.ShapeDtypeStruct((1, ROWS), F32)),
        in_specs=[vmem] * 9,
        out_specs=(vmem, vmem),
        scratch_shapes=[
            pltpu.VMEM((8, ROWS, FEATURES), BF16),
            pltpu.VMEM((8, 2 * ROWS, QKV), BF16),
            pltpu.VMEM((2, 8, ROWS, 512), BF16),
            pltpu.VMEM((8, ROWS, 512), BF16),
            pltpu.VMEM((2, 16 * CAP, 512), BF16),
            pltpu.VMEM((2, 16 * CAP, 512), BF16),
            pltpu.VMEM((ROWS, 512), BF16),
            pltpu.VMEM((ROWS, QKV), F32),
            pltpu.VMEM((ROWS, QKV), BF16),
            pltpu.VMEM((ROWS, FEATURES), F32),
            pltpu.VMEM((8, 8, ROWS), F32),
            pltpu.VMEM((ROWS, 128), F32),
            pltpu.VMEM((16, ROWS), jnp.int32),
            pltpu.VMEM((ROWS, 384), F32),
            pltpu.VMEM((8, 16 * CAP), jnp.int32),
            pltpu.VMEM((16, 8, 128), F32),
            pltpu.VMEM((16, 8, 128), F32),
            pltpu.VMEM((8, 64, 512), BF16),
            dma((7 * H_PIECES,)), dma((8, H_PIECES)),
            dma((15 * W_PIECES,)), dma((16, W_PIECES)),
            dma((60,)), dma((16, 4)),
            dma((8,)), dma((8,)),
            dma((7 * A_PIECES,)), dma((8, A_PIECES)),
            dma((2, 16)), dma((2, 16)),
            dma((8,)), dma((8,)),
            dma((16,)), dma((16,)),
            dma((8,)), dma((8,)),
        ],
        compiler_params=pltpu.CompilerParams(
            collective_id=0, has_side_effects=True, vmem_limit_bytes=58 * 2**20
        ),
        name="layer",
    )(
        hidden_in, assignment, attn_gain, value_head, w_query, w_key, w_value_proj, w_out,
        jnp.asarray(rotary_table()),
    )
    return scored, values.reshape(ROWS)


def solution(mesh):
    in_specs = (P("zero", "tp"), P(), P(), P("zero", "tp"), P("zero", "tp"), P("zero", "tp"), P("tp", "zero"), P())
    return jax.shard_map(
        shards, mesh=mesh, in_specs=in_specs, out_specs=(P("zero", "tp"), P("zero")), check_vma=False
    )
```
